512 devices in a mesh: row: 16 (over x_lo, z), col: 32 (over y, x_hi, core).
Axes of the slice: x: 4 (x_hi: 2, x_lo: 2; x = x_hi * 2 + x_lo), y: 8, z: 8, core: 2. Of those that a mesh axis runs over, the one named last changes fastest.
Arguments:
- activations: bfloat16 [512, 32768], P('row', 'col'), may hold values from -6 to 6
- conv_one: bfloat16 [3, 3, 64, 64], replicated, may hold values from -0.25 to 0.25
- bias_one: float32 [64], replicated, may hold values from -3 to 3
- conv_two: bfloat16 [3, 3, 64, 64], replicated, may hold values from -0.25 to 0.25
- bias_two: float32 [64], replicated, may hold values from -3 to 3
- cotangent: bfloat16 [512, 32768], P('row', 'col'), may hold values from -6 to 6
Outputs:
- symmetric_out: bfloat16 [512, 32768], P('row', 'col')
- input_grad: bfloat16 [512, 32768], P('row', 'col')
- grad_w1: float32 [3, 3, 64, 64], replicated
- grad_b1: float32 [64], replicated
- grad_w2: float32 [3, 3, 64, 64], replicated
- grad_b2: float32 [64], replicated
The draws below stay inside these ranges and needn't reach their ends.
All inputs are finite; a program needn't handle non-finite values.
Results may differ from the reference program's by a relative error of at most 0.01.
Values may be sent and summed in bfloat16 or wider, within the bound.
A program may use at most 64 MiB of HBM per device.

```python
import jax
import jax.numpy as jnp
from jax import lax

CH = 64
DILATION = 4
BINS = 512


def block_scale(own_key, extent, pieces, smallest, top_value):
    def one(axis_at, blocks):
        heights = jax.random.uniform(jax.random.fold_in(jax.random.fold_in(own_key, 6), axis_at), (blocks,), jnp.float32, smallest / len(pieces), top_value / len(pieces))
        return jnp.repeat(jnp.exp(heights), extent[axis_at] // blocks).reshape((-1,) + (1,) * (len(extent) - axis_at - 1))

    factor_of = one(*pieces[0])
    for cut in pieces[1:]:
        factor_of = factor_of * one(*cut)
    return factor_of


def bell_draw(stream_key, dims, spread, reach, split=(), kind=jnp.bfloat16):
    level = block_scale(stream_key, dims, split, -0.22, 0.18) if split else 1.0
    entries = jax.random.normal(stream_key, dims, jnp.float32) * spread * level
    return jnp.minimum(jnp.maximum(entries, -reach), reach).astype(kind)


def setup_inputs(seed: int = 0) -> dict:
    key_of = jax.random.split(jax.random.key(seed), 7)
    return {
        "activations": bell_draw(key_of[0], (BINS, BINS * CH), 1.0, 6.0, ((0, 16), (1, 32))),
        "conv_one": bell_draw(key_of[1], (3, 3, CH, CH), (9 * CH) ** -0.5, 0.25),
        "bias_one": bell_draw(key_of[2], (CH,), 0.5, 3.0, (), jnp.float32),
        "conv_two": bell_draw(key_of[3], (3, 3, CH, CH), (9 * CH) ** -0.5, 0.25),
        "bias_two": bell_draw(key_of[4], (CH,), 0.5, 3.0, (), jnp.float32),
        "cotangent": bell_draw(key_of[5], (BINS, BINS * CH), 1.0, 6.0, ((0, 16), (1, 32))),
    }


def activate(values):
    return jax.nn.gelu(values, approximate=True)

def dilated_same(source, kernel):
    return lax.conv_general_dilated(source.astype(jnp.float32)[None], kernel.astype(jnp.float32), (1, 1), ((DILATION, DILATION), (DILATION, DILATION)), rhs_dilation=(DILATION, DILATION), dimension_numbers=('NHWC', 'HWIO', 'NHWC'), precision=lax.Precision.HIGHEST)[0]

def flipped(kernel):
    return jnp.swapaxes(kernel[::-1, ::-1], 2, 3)

def kernel_grad(source, out_grad):
    padded = jnp.pad(source.astype(jnp.float32), ((DILATION, DILATION), (DILATION, DILATION), (0, 0)))
    grad_f = out_grad.astype(jnp.float32)
    rows_out = []
    for tap_row in range(3):
        cols_out = []
        for tap_col in range(3):
            window = lax.slice(padded, (tap_row * DILATION, tap_col * DILATION, 0), (tap_row * DILATION + BINS, tap_col * DILATION + BINS, CH))
            cols_out.append(jnp.einsum('rci,rco->io', window, grad_f, precision=lax.Precision.HIGHEST))
        rows_out.append(jnp.stack(cols_out))
    return jnp.stack(rows_out)

def symmetric(field_in):
    values = field_in.astype(jnp.float32)
    return ((values + jnp.swapaxes(values, 0, 1)) * 0.5).astype(jnp.bfloat16)

def reference(activations, conv_one, bias_one, conv_two, bias_two, cotangent):
    source = activations.reshape(BINS, BINS, CH)
    preact = dilated_same(source, conv_one) + bias_one
    hidden = activate(preact).astype(jnp.bfloat16)
    summed = (source.astype(jnp.float32) + dilated_same(hidden, conv_two) + bias_two).astype(jnp.bfloat16)
    symmetric_out = symmetric(summed)
    sym_grad = symmetric(cotangent.reshape(BINS, BINS, CH))
    hid_grad = dilated_same(sym_grad, flipped(conv_two))
    pre_grad = jax.vjp(activate, preact)[1](hid_grad)[0].astype(jnp.bfloat16)
    input_grad = (sym_grad.astype(jnp.float32) + dilated_same(pre_grad, flipped(conv_one))).astype(jnp.bfloat16)
    inv_bins = 1.0 / BINS
    grad_w1 = kernel_grad(source, pre_grad) * inv_bins
    grad_b1 = lax.optimization_barrier(jnp.sum(pre_grad.astype(jnp.float32), axis=(0, 1))) * inv_bins
    grad_w2 = kernel_grad(hidden, sym_grad) * inv_bins
    grad_b2 = lax.optimization_barrier(jnp.sum(sym_grad.astype(jnp.float32), axis=(0, 1))) * inv_bins
    return (symmetric_out.reshape(BINS, BINS * CH), input_grad.reshape(BINS, BINS * CH), grad_w1, grad_b1, grad_w2, grad_b2)
```

```python
import jax
import jax.numpy as jnp
from jax import lax
from jax.experimental import pallas as pl
from jax.experimental.pallas import tpu as pltpu
from jax.sharding import PartitionSpec as P

DILATION = 4
MESH = pl.DeviceIdType.MESH
WIDE = 8
PLANE = 64
OWNERS = 10
ROWS = 72
PIECE = 80


def place():
    row = lax.axis_index("row")
    col = lax.axis_index("col")
    near = lax.rem(col, 4) * 2 + row // 8
    far = (col // 4) * 8 + lax.rem(row, 8)
    return row, col, near, far


def near_id(row, col, peer):
    return (lax.rem(peer, 2) * 8 + lax.rem(row, 8), (col // 4) * 4 + peer // 2)


def far_id(row, col, peer):
    return ((row // 8) * 8 + lax.rem(peer, 8), (peer // 8) * 4 + lax.rem(col, 4))


def reduce_kernel(parts, full, got_a, mine, got_b, total, a_send, a_recv, b_send, b_recv, t_send, t_recv, c_send, c_recv):
    row, col, near, far = place()
    lead = far - near
    owned = lead // 6
    is_owner = (lead >= 0) & (lax.rem(lead, 6) == 0) & (owned < OWNERS)

    barrier = pltpu.get_barrier_semaphore()
    for step in range(1, WIDE):
        pl.semaphore_signal(barrier, inc=1, device_id=near_id(row, col, lax.rem(near + step, WIDE)), device_id_type=MESH)
    for tile in range(OWNERS):
        owner = 6 * tile + near

        @pl.when(owner != far)
        def _():
            pl.semaphore_signal(barrier, inc=1, device_id=far_id(row, col, owner), device_id_type=MESH)

    @pl.when(is_owner)
    def _():
        @pl.loop(1, PLANE)
        def _(step):
            pl.semaphore_signal(barrier, inc=1, device_id=far_id(row, col, lax.rem(far + step, PLANE)), device_id_type=MESH)

    pl.semaphore_wait(barrier, WIDE - 1 + OWNERS + jnp.where(is_owner, PLANE - 2, 0))

    sends = []
    for step in range(1, WIDE):
        peer = lax.rem(near + step, WIDE)
        copy = pltpu.make_async_remote_copy(
            src_ref=parts.at[peer],
            dst_ref=got_a.at[step - 1],
            send_sem=a_send.at[step - 1],
            recv_sem=a_recv.at[step - 1],
            device_id=near_id(row, col, peer),
            device_id_type=MESH,
        )
        copy.start()
        sends.append(copy)
    acc = parts[near]
    for step in range(1, WIDE):
        sends[step - 1].wait_recv()
        acc = acc + got_a[step - 1]
    mine[...] = acc.reshape(OWNERS, 8, 128)

    for tile in range(OWNERS):
        owner = 6 * tile + near

        @pl.when(owner != far)
        def _():
            pltpu.make_async_remote_copy(
                src_ref=mine.at[tile],
                dst_ref=got_b.at[far],
                send_sem=b_send,
                recv_sem=b_recv,
                device_id=far_id(row, col, owner),
                device_id_type=MESH,
            ).start()

    @pl.when(is_owner)
    def _():
        got_b[far] = mine[owned]
        pltpu.make_async_copy(got_b.at[pl.ds(0, PLANE - 1)], got_b.at[pl.ds(0, PLANE - 1)], b_recv).wait()
        total[owned] = jnp.sum(got_b[...], axis=0)

        @pl.loop(1, PLANE)
        def _(step):
            pltpu.make_async_remote_copy(
                src_ref=total.at[owned],
                dst_ref=total.at[owned],
                send_sem=t_send,
                recv_sem=t_recv,
                device_id=far_id(row, col, lax.rem(far + step, PLANE)),
                device_id_type=MESH,
            ).start()

        pltpu.make_async_copy(total.at[pl.ds(0, OWNERS - 1)], total.at[pl.ds(0, OWNERS - 1)], t_recv).wait()

    @pl.when(jnp.logical_not(is_owner))
    def _():
        pltpu.make_async_copy(total, total, t_recv).wait()

    lasts = []
    for step in range(1, WIDE):
        peer = lax.rem(near + step, WIDE)
        copy = pltpu.make_async_remote_copy(
            src_ref=total,
            dst_ref=full.at[near],
            send_sem=c_send.at[step - 1],
            recv_sem=c_recv.at[step - 1],
            device_id=near_id(row, col, peer),
            device_id_type=MESH,
        )
        copy.start()
        lasts.append(copy)
    full[near] = total[...]
    for copy in sends:
        copy.wait_send()

    @pl.when(is_owner)
    def _():
        pltpu.make_async_copy(total.at[pl.ds(0, OWNERS - 1)], total.at[pl.ds(0, OWNERS - 1)], b_send).wait()
        pltpu.make_async_copy(got_b.at[pl.ds(0, PLANE - 1)], got_b.at[pl.ds(0, PLANE - 1)], t_send).wait()

    @pl.when(jnp.logical_not(is_owner))
    def _():
        pltpu.make_async_copy(total, total, b_send).wait()

    for copy in lasts:
        copy.wait()


def reduce_all(parts):
    return pl.pallas_call(
        reduce_kernel,
        out_shape=jax.ShapeDtypeStruct((WIDE, OWNERS, 8, 128), jnp.float32),
        in_specs=[pl.BlockSpec(memory_space=pltpu.VMEM)],
        out_specs=pl.BlockSpec(memory_space=pltpu.VMEM),
        scratch_shapes=[
            pltpu.VMEM((WIDE - 1, PIECE, 128), jnp.float32),
            pltpu.VMEM((OWNERS, 8, 128), jnp.float32),
            pltpu.VMEM((PLANE, 8, 128), jnp.float32),
            pltpu.VMEM((OWNERS, 8, 128), jnp.float32),
            pltpu.SemaphoreType.DMA((WIDE - 1,)),
            pltpu.SemaphoreType.DMA((WIDE - 1,)),
            pltpu.SemaphoreType.DMA,
            pltpu.SemaphoreType.DMA,
            pltpu.SemaphoreType.DMA,
            pltpu.SemaphoreType.DMA,
            pltpu.SemaphoreType.DMA((WIDE - 1,)),
            pltpu.SemaphoreType.DMA((WIDE - 1,)),
        ],
        compiler_params=pltpu.CompilerParams(collective_id=0, has_side_effects=True),
    )(parts)


def padded_2(cells, sides, width):
    for axis, dim in sides:
        count = lax.axis_size(axis)
        ends = count - 1
        head = lax.slice_in_dim(cells, 0, width, axis=dim)
        tail = lax.slice_in_dim(cells, cells.shape[dim] - width, cells.shape[dim], axis=dim)
        cells = jnp.concatenate(
            [
                lax.ppermute(tail, axis, [(i, (i + 1) % count) for i in range(ends)]),
                cells,
                lax.ppermute(head, axis, [((i + 1) % count, i) for i in range(ends)]),
            ],
            axis=dim,
        )
    return cells


def activate(values):
    return jax.nn.gelu(values, approximate=True)


def dilated(padded, kernel):
    return lax.conv_general_dilated(
        padded[None],
        kernel,
        (1, 1),
        "VALID",
        rhs_dilation=(DILATION, DILATION),
        dimension_numbers=("NHWC", "HWIO", "NHWC"),
        preferred_element_type=jnp.float32,
    )[0]


def flipped(kernel):
    return jnp.swapaxes(kernel[::-1, ::-1], 2, 3)


def kernel_grad(padded, out_grad):
    row_count, col_count, channels = out_grad.shape
    rows_out = []
    for tap_row in range(3):
        cols_out = []
        for tap_col in range(3):
            window = lax.slice(
                padded,
                (tap_row * DILATION, tap_col * DILATION, 0),
                (tap_row * DILATION + row_count, tap_col * DILATION + col_count, padded.shape[2]),
            )
            cols_out.append(
                jnp.einsum("rci,rco->io", window, out_grad, preferred_element_type=jnp.float32)
            )
        rows_out.append(jnp.stack(cols_out))
    return jnp.stack(rows_out)


def mirror_tile(patch_in):
    col_total = lax.axis_size("col")
    row_total = lax.axis_size("row")
    fold_ratio = col_total // row_total
    row_count, col_count, channels = patch_in.shape
    blocks = patch_in.reshape(fold_ratio, col_count * col_count * channels)
    sectioned = blocks.reshape(fold_ratio, col_total, -1)
    sectioned = lax.all_to_all(
        lax.all_to_all(sectioned, "col", split_axis=1, concat_axis=1, tiled=True),
        "row",
        split_axis=1,
        concat_axis=0,
        tiled=True,
    )
    sectioned = lax.all_to_all(sectioned, "col", split_axis=0, concat_axis=0, tiled=True)
    mirrored = jnp.swapaxes(sectioned, 0, 1)
    mirrored = mirrored.reshape(fold_ratio, col_count, col_count, channels)
    return jnp.swapaxes(mirrored, 1, 2).reshape(row_count, col_count, channels)


def symmetric(patch_in):
    values = patch_in.astype(jnp.float32) + mirror_tile(patch_in).astype(jnp.float32)
    return (values * 0.5).astype(jnp.bfloat16)


def on_device(activations, conv_one, bias_one, conv_two, bias_two, cotangent):
    channels = conv_one.shape[2]
    row_count = activations.shape[0]
    col_count = activations.shape[1] // channels
    source = activations.reshape(row_count, col_count, channels)
    padded_in = padded_2(source, (("row", 0), ("col", 1)), DILATION)
    preact = dilated(padded_in, conv_one) + bias_one
    hidden = activate(preact).astype(jnp.bfloat16)
    hidden_pad = padded_2(hidden, (("row", 0), ("col", 1)), DILATION)
    branch = dilated(hidden_pad, conv_two) + bias_two
    summed = (source.astype(jnp.float32) + branch).astype(jnp.bfloat16)
    symmetric_out = symmetric(summed)
    sym_grad = symmetric(cotangent.reshape(row_count, col_count, channels))
    grad_pad = padded_2(sym_grad, (("row", 0), ("col", 1)), DILATION)
    hid_grad = dilated(grad_pad, flipped(conv_two))
    pre_grad = jax.vjp(activate, preact)[1](hid_grad)[0].astype(jnp.bfloat16)
    pre_pad = padded_2(pre_grad, (("row", 0), ("col", 1)), DILATION)
    input_grad = (sym_grad.astype(jnp.float32) + dilated(pre_pad, flipped(conv_one))).astype(
        jnp.bfloat16
    )
    inv_bins = 1.0 / (row_count * lax.axis_size("row"))
    taps = jnp.concatenate(
        [
            kernel_grad(padded_in, pre_grad).reshape(9 * channels, channels),
            kernel_grad(hidden_pad, sym_grad).reshape(9 * channels, channels),
        ],
        axis=1,
    )
    biases = jnp.concatenate(
        [
            jnp.sum(pre_grad, axis=(0, 1), dtype=jnp.float32),
            jnp.sum(sym_grad, axis=(0, 1), dtype=jnp.float32),
        ]
    )
    parts = jnp.concatenate(
        [taps.reshape(WIDE, ROWS, 128), jnp.broadcast_to(biases, (WIDE, 8, 128))], axis=1
    )
    full = reduce_all(parts * inv_bins).reshape(WIDE, PIECE, 128)
    taps = full[:, :ROWS].reshape(3, 3, channels, 2 * channels)
    biases = full[0, ROWS]
    totals = (
        taps[..., :channels],
        biases[:channels],
        taps[..., channels:],
        biases[channels:],
    )
    return (
        symmetric_out.reshape(row_count, col_count * channels),
        input_grad.reshape(row_count, col_count * channels),
        totals[0],
        totals[1],
        totals[2],
        totals[3],
    )


def solution(mesh):
    return jax.shard_map(
        on_device,
        mesh=mesh,
        in_specs=(P("row", "col"), P(), P(), P(), P(), P("row", "col")),
        out_specs=(P("row", "col"), P("row", "col"), P(), P(), P(), P()),
        check_vma=False,
    )
```

```python
import jax
import jax.numpy as jnp
from jax import lax
from jax.experimental import pallas as pl
from jax.experimental.pallas import tpu as pltpu
from jax.sharding import PartitionSpec as P

MESH = pl.DeviceIdType.MESH
F32 = jnp.float32
BF16 = jnp.bfloat16
CH = 64
ROWS = 32
WIDTH = 1024
QUAD = 256
INV_BINS = 1.0 / 512
PLANE = 32
DEPTH = 8
LINES = 10
SLOPE = 0.7978845608
CUBIC = 0.044715
AROUND = tuple((a, b) for a in (-1, 0, 1) for b in (-1, 0, 1) if a or b)
ENDS = {-1: (pl.ds(1, 1), pl.ds(5, 1)), 0: (pl.ds(1, 4), pl.ds(1, 4)), 1: (pl.ds(4, 1), pl.ds(0, 1))}
SIDES = {-1: (pl.ds(1, 1), pl.ds(3, 1)), 0: (pl.ds(1, 2), pl.ds(1, 2)), 1: (pl.ds(2, 1), pl.ds(0, 1))}


def plane_id(row, col, peer):
    return (lax.rem(peer, 2) * 8 + lax.rem(row, 8), (peer // 2) * 2 + lax.rem(col, 2))


def depth_id(row, col, peer):
    return ((row // 8) * 8 + peer, col)


def block_of(taps, transpose):
    zero = jnp.zeros((CH, CH), F32)
    value = taps.astype(F32)
    if transpose:
        value = value.T
    left = jnp.concatenate([value, zero], axis=1).astype(BF16)
    right = jnp.concatenate([zero, value], axis=1).astype(BF16)
    return left, right


def fill(matrix, taps_ref, flip):
    matrix[...] = jnp.zeros(matrix.shape, BF16)
    for a in range(3):
        for b in range(3):
            if flip:
                left, right = block_of(taps_ref[2 - a, 2 - b], True)
            else:
                left, right = block_of(taps_ref[a, b], False)
            for k in range(4):
                rows = pl.ds(b * QUAD + k * CH, CH)
                cols = pl.ds(a * QUAD + (k // 2) * 128, 128)
                matrix[rows, cols] = right if k % 2 else left


def pack(own, padded):
    for q in range(4):
        for g in range(2):
            rows = own[8 * q : 8 * q + 8]
            pair = [rows[:, QUAD * (2 * g + s) : QUAD * (2 * g + s + 1)] for s in range(2)]
            padded[q + 1, g + 1] = jnp.concatenate(pair, axis=0).astype(BF16)


def unpack(padded):
    values = padded[...].astype(F32)
    return [
        jnp.concatenate([values[q, g // 2, 8 * (g % 2) : 8 * (g % 2) + 8] for q in range(6)], axis=0).astype(BF16)
        for g in range(8)
    ]


def clear_edges(padded, row, col):
    @pl.when(row == 0)
    def _():
        padded[0] = jnp.zeros((4, 16, QUAD), BF16)

    @pl.when(row == 15)
    def _():
        padded[5] = jnp.zeros((4, 16, QUAD), BF16)

    @pl.when(col == 0)
    def _():
        padded[:, 0] = jnp.zeros((6, 16, QUAD), BF16)

    @pl.when(col == 31)
    def _():
        padded[:, 3] = jnp.zeros((6, 16, QUAD), BF16)


def conv(groups, matrix, rows):
    count = len(groups) - 2
    left = jnp.concatenate([jnp.stack(groups[b : b + count]) for b in range(3)], axis=-1)
    full = jnp.dot(left.reshape(count * 48, 3 * QUAD), matrix[...], preferred_element_type=F32)
    full = full.reshape(count, 48, 3 * QUAD)
    return (
        full[:, 0:rows, 0:QUAD]
        + full[:, 4 : 4 + rows, QUAD : 2 * QUAD]
        + full[:, 8 : 8 + rows, 2 * QUAD :]
    )


def taps_of(groups, grads):
    count, rows = grads.shape[:2]
    shifted = []
    for a in range(3):
        parts = [grads]
        if a:
            parts.insert(0, jnp.zeros((count, 4 * a, QUAD), F32))
        if 48 - rows - 4 * a:
            parts.append(jnp.zeros((count, 48 - rows - 4 * a, QUAD), F32))
        shifted.append(jnp.concatenate(parts, axis=1) if len(parts) > 1 else grads)
    right = jnp.concatenate(shifted, axis=-1).astype(BF16).reshape(count * 48, 3 * QUAD)
    out = []
    for b in range(3):
        left = jnp.stack(groups[b : b + count]).reshape(count * 48, QUAD)
        out.append(lax.dot_general(left, right, (((0,), (0,)), ((), ())), preferred_element_type=F32))
    return out


def halves(full, a):
    one = full[:, a * QUAD : a * QUAD + 128]
    two = full[:, a * QUAD + 128 : (a + 1) * QUAD]
    return one[0:64] + two[128:192], one[64:128] + two[192:256]


def turned(block, spare, base):
    lane = lax.broadcasted_iota(jnp.int32, (8, 128), 1)
    for p in range(8):
        spare[pl.ds(base + 16 * p, 16), :] = block[:, 128 * p : 128 * p + 128]
    for p in range(8):
        even = spare[pl.ds(base + 16 * p, 8, stride=2), :]
        odd = spare[pl.ds(base + 16 * p + 1, 8, stride=2), :]
        spare[pl.ds(base + 128 + 16 * p, 8), :] = jnp.where(lane < 64, even, pltpu.roll(odd, 64, 1))
        spare[pl.ds(base + 128 + 16 * p + 8, 8), :] = jnp.where(lane < 64, pltpu.roll(even, 64, 1), odd)
    return jnp.concatenate([spare[pl.ds(base + 128 + q, 16, stride=8), :] for q in range(8)], axis=1)


def grouped(tile):
    return jnp.stack([tile[:, QUAD * g : QUAD * (g + 1)] for g in range(4)])


def kernel(
    act_hbm, cot_hbm, one_hbm, two_hbm, bias_one, bias_two,
    sym_out, grad_out, full,
    act, cot, one, two, mat_one, mat_two, back_one, back_two,
    source_pad, sym_pad, mirror, summed, mirror_sum, spare,
    parts, core_in, plane_in, depth_in, piece,
    load_sem, m_send, m_recv, s_send, s_recv, x_send, x_recv, g_send, g_recv, ar_send, ar_recv,
):
    row, col = lax.axis_index("row"), lax.axis_index("col")
    core = lax.rem(col, 2)
    plane = (col // 2) * 2 + row // 8
    depth = lax.rem(row, 8)
    sibling = (row, col + 1 - 2 * core)
    around = [(lax.rem(row + a + 16, 16), lax.rem(col + b + 32, 32)) for a, b in AROUND]
    opposite = [(col // 2, 2 * row + h) for h in range(2)]
    diagonal = col // 2 == row
    is_self = [diagonal & (core == h) for h in range(2)]

    barrier = pltpu.get_barrier_semaphore()
    for h in range(2):
        @pl.when(jnp.logical_not(is_self[h]))
        def _():
            pl.semaphore_signal(barrier, inc=1, device_id=opposite[h], device_id_type=MESH)
    for device in around + [sibling]:
        pl.semaphore_signal(barrier, inc=1, device_id=device, device_id_type=MESH)

    @pl.loop(1, PLANE)
    def _(step):
        pl.semaphore_signal(barrier, inc=1, device_id=plane_id(row, col, lax.rem(plane + step, PLANE)), device_id_type=MESH)

    @pl.loop(1, DEPTH)
    def _(step):
        pl.semaphore_signal(barrier, inc=1, device_id=depth_id(row, col, lax.rem(depth + step, DEPTH)), device_id_type=MESH)

    loads = [
        pltpu.make_async_copy(src, dst, load_sem.at[k])
        for k, (src, dst) in enumerate(((act_hbm, act), (one_hbm, one), (two_hbm, two), (cot_hbm, cot)))
    ]
    for copy in loads:
        copy.start()
    loads[0].wait()
    source = act[...].astype(F32)
    pack(source, source_pad)

    def swap_start(src, dst, send, recv):
        for h in range(2):
            @pl.when(jnp.logical_not(is_self[h]))
            def _():
                pltpu.make_async_remote_copy(
                    src_ref=src.at[pl.ds(16 * h, 16)], dst_ref=dst.at[core], send_sem=send.at[h], recv_sem=recv.at[core],
                    device_id=opposite[h], device_id_type=MESH,
                ).start()

            @pl.when(is_self[h])
            def _():
                pltpu.make_async_copy(src.at[pl.ds(16 * h, 16)], dst.at[core], recv.at[core]).start()

    def swap_sent(src, dst, send):
        for h in range(2):
            @pl.when(jnp.logical_not(is_self[h]))
            def _():
                pltpu.make_async_copy(src.at[pl.ds(16 * h, 16)], dst.at[h], send.at[h]).wait()

    def halo_start(padded, send, recv):
        copies = []
        for k, (a, b) in enumerate(AROUND):
            copies.append(
                pltpu.make_async_remote_copy(
                    src_ref=padded.at[ENDS[a][0], SIDES[b][0]], dst_ref=padded.at[ENDS[a][1], SIDES[b][1]],
                    send_sem=send.at[k], recv_sem=recv.at[k], device_id=around[k], device_id_type=MESH,
                )
            )
            copies[-1].start()
        return copies

    pl.semaphore_wait(barrier, 2 + 8 + 1 + PLANE - 1 + DEPTH - 1 - diagonal.astype(jnp.int32))
    swap_start(cot_hbm, mirror, m_send, m_recv)
    source_halo = halo_start(source_pad, s_send, s_recv)

    loads[1].wait()
    loads[2].wait()
    fill(mat_one, one, False)
    fill(mat_two, two, False)
    fill(back_two, two, True)
    fill(back_one, one, True)
    parts[8:CH, 9, :] = jnp.zeros((CH - 8, 128), F32)

    line = lax.broadcasted_iota(jnp.int32, (40, QUAD), 0)
    inside = ((line >= 4) | (row > 0)) & ((line < 36) | (row < 15))
    first = inside & (col > 0)
    last = inside & (col < 31)

    def masked(values):
        return jnp.stack([jnp.where((first, inside, inside, inside, inside, last)[g], values[g], 0.0) for g in range(6)])

    for copy in source_halo:
        copy.wait_recv()
    clear_edges(source_pad, row, col)
    source_groups = unpack(source_pad)
    wide_one = jnp.concatenate([bias_one[...]] * 4, axis=1)
    wide_two = jnp.concatenate([bias_two[...]] * 4, axis=1)
    preact = conv(source_groups, mat_one, 40) + wide_one
    bent = jnp.tanh(SLOPE * (preact + CUBIC * preact * preact * preact))
    hidden = masked(0.5 * preact * (1.0 + bent))
    slope = masked(
        0.5 * (1.0 + bent)
        + 0.5 * preact * (1.0 - bent * bent) * (SLOPE * (1.0 + 3.0 * CUBIC * preact * preact))
    )
    blank = jnp.zeros((6, 8, QUAD), F32)
    hidden = jnp.concatenate([hidden, blank], axis=1).astype(BF16)
    hidden_groups = [hidden[g] for g in range(6)]
    branch = conv(hidden_groups, mat_two, 32) + wide_two
    summed[...] = (source + jnp.concatenate([branch[g] for g in range(4)], axis=1)).astype(BF16)

    loads[3].wait()
    for h in range(2):
        pltpu.make_async_copy(mirror.at[h], mirror.at[h], m_recv.at[h]).wait()
    turned_cot = jnp.concatenate([turned(mirror[h].astype(F32), spare, 256 * h) for h in range(2)], axis=0)
    sym = ((cot[...].astype(F32) + turned_cot) * 0.5).astype(BF16).astype(F32)
    pack(sym, sym_pad)
    sym_halo = halo_start(sym_pad, g_send, g_recv)
    swap_start(summed, mirror_sum, x_send, x_recv)

    sym_own = grouped(sym)
    lower = jnp.zeros((4, 8, QUAD), F32)
    sym_rows = jnp.concatenate([lower, sym_own, lower], axis=1).astype(BF16)
    nothing = jnp.zeros((48, QUAD), BF16)
    sym_groups = [nothing] * 2 + [sym_rows[g] for g in range(4)] + [nothing] * 2
    share = conv(sym_groups, back_two, 40) * slope
    taps_two = taps_of(hidden_groups, sym_own)
    taps_one = taps_of(source_groups, share)
    left = lax.broadcasted_iota(jnp.int32, (CH, 128), 1) < CH
    for a in range(3):
        for b in range(3):
            near_one, far_one = halves(taps_one[b], a)
            near_two, far_two = halves(taps_two[b], a)
            parts[:, 3 * a + b, :] = jnp.where(
                left, near_one + pltpu.roll(far_one, CH, 1), far_two + pltpu.roll(near_two, CH, 1)
            )
    bias = []
    for grads in (share, sym_own):
        total = jnp.sum(grads.reshape(-1, 8, QUAD), axis=0)
        total = total[:, :128] + total[:, 128:]
        bias.append(total + pltpu.roll(total, CH, 1))
    parts[0:8, 9, :] = jnp.where(left[:8], bias[0], bias[1])

    own = pl.ds(PLANE * core, PLANE)
    to_core = pltpu.make_async_remote_copy(
        src_ref=parts.at[pl.ds(PLANE * (1 - core), PLANE)], dst_ref=core_in, send_sem=ar_send.at[0], recv_sem=ar_recv.at[0],
        device_id=sibling, device_id_type=MESH,
    )
    to_core.start()
    to_core.wait_recv()
    core_in[...] = core_in[...] + parts[own]

    @pl.loop(1, PLANE)
    def _(step):
        peer = lax.rem(plane + step, PLANE)
        pltpu.make_async_remote_copy(
            src_ref=core_in.at[peer], dst_ref=plane_in.at[step - 1], send_sem=ar_send.at[1], recv_sem=ar_recv.at[1],
            device_id=plane_id(row, col, peer), device_id_type=MESH,
        ).start()

    for copy in sym_halo:
        copy.wait_recv()
    clear_edges(sym_pad, row, col)
    pre_grad = conv(unpack(sym_pad), back_two, 40) * slope
    pre_grad = jnp.concatenate([pre_grad, blank], axis=1).astype(BF16)
    input_grad = conv([pre_grad[g] for g in range(6)], back_one, 32)
    grad_out[...] = (sym + jnp.concatenate([input_grad[g] for g in range(4)], axis=1)).astype(BF16)

    pltpu.make_async_copy(plane_in, plane_in, ar_recv.at[1]).wait()
    depth_in[depth] = jnp.sum(plane_in[...], axis=0) + core_in[plane]

    @pl.loop(1, DEPTH)
    def _(step):
        peer = lax.rem(depth + step, DEPTH)
        pltpu.make_async_remote_copy(
            src_ref=depth_in.at[depth], dst_ref=depth_in.at[depth], send_sem=ar_send.at[2], recv_sem=ar_recv.at[2],
            device_id=depth_id(row, col, peer), device_id_type=MESH,
        ).start()

    for h in range(2):
        pltpu.make_async_copy(mirror_sum.at[h], mirror_sum.at[h], x_recv.at[h]).wait()
    turned_sum = jnp.concatenate([turned(mirror_sum[h].astype(F32), spare, 256 * h) for h in range(2)], axis=0)
    sym_out[...] = ((summed[...].astype(F32) + turned_sum) * 0.5).astype(BF16)

    pltpu.make_async_copy(depth_in.at[pl.ds(0, DEPTH - 1)], depth_in.at[pl.ds(0, DEPTH - 1)], ar_recv.at[2]).wait()
    here = PLANE * core + plane
    full[here] = jnp.sum(depth_in[...], axis=0) * INV_BINS

    @pl.loop(1, PLANE)
    def _(step):
        pltpu.make_async_remote_copy(
            src_ref=full.at[here], dst_ref=full.at[here], send_sem=ar_send.at[3], recv_sem=ar_recv.at[3],
            device_id=plane_id(row, col, lax.rem(plane + step, PLANE)), device_id_type=MESH,
        ).start()

    pltpu.make_async_copy(plane_in, plane_in, ar_recv.at[3]).wait()
    back_core = pltpu.make_async_remote_copy(
        src_ref=full.at[own], dst_ref=full.at[own], send_sem=ar_send.at[4], recv_sem=ar_recv.at[4],
        device_id=sibling, device_id_type=MESH,
    )
    back_core.start()
    swap_sent(cot_hbm, mirror, m_send)
    swap_sent(summed, mirror_sum, x_send)
    for copy in source_halo + sym_halo + [to_core]:
        copy.wait_send()
    pltpu.make_async_copy(plane_in, plane_in, ar_send.at[1]).wait()
    pltpu.make_async_copy(depth_in.at[pl.ds(0, DEPTH - 1)], depth_in.at[pl.ds(0, DEPTH - 1)], ar_send.at[2]).wait()
    pltpu.make_async_copy(plane_in, plane_in, ar_send.at[3]).wait()
    back_core.wait()


def on_device(activations, conv_one, bias_one, conv_two, bias_two, cotangent):
    vmem, anywhere = pl.BlockSpec(memory_space=pltpu.VMEM), pl.BlockSpec(memory_space=pl.ANY)
    dma = pltpu.SemaphoreType.DMA
    tile = jax.ShapeDtypeStruct((ROWS, WIDTH), BF16)
    symmetric_out, input_grad, full = pl.pallas_call(
        kernel,
        out_shape=(tile, tile, jax.ShapeDtypeStruct((CH, LINES, 128), F32)),
        in_specs=[anywhere] * 4 + [vmem] * 2,
        out_specs=[vmem] * 3,
        scratch_shapes=[
            pltpu.VMEM((ROWS, WIDTH), BF16),
            pltpu.VMEM((ROWS, WIDTH), BF16),
            pltpu.VMEM((3, 3, CH, CH), BF16),
            pltpu.VMEM((3, 3, CH, CH), BF16),
        ]
        + [pltpu.VMEM((3 * QUAD, 3 * QUAD), BF16)] * 4
        + [
            pltpu.VMEM((6, 4, 16, QUAD), BF16),
            pltpu.VMEM((6, 4, 16, QUAD), BF16),
            pltpu.VMEM((2, 16, WIDTH), BF16),
            pltpu.VMEM((ROWS, WIDTH), BF16),
            pltpu.VMEM((2, 16, WIDTH), BF16),
            pltpu.VMEM((512, 128), F32),
            pltpu.VMEM((CH, LINES, 128), F32),
            pltpu.VMEM((PLANE, LINES, 128), F32),
            pltpu.VMEM((PLANE - 1, LINES, 128), F32),
            pltpu.VMEM((DEPTH, LINES, 128), F32),
            pltpu.VMEM((LINES, 128), F32),
            dma((4,)), dma((2,)), dma((2,)), dma((8,)), dma((8,)), dma((2,)), dma((2,)), dma((8,)), dma((8,)), dma((5,)), dma((5,)),
        ],
        compiler_params=pltpu.CompilerParams(collective_id=0, has_side_effects=True, vmem_limit_bytes=48 * 1024 * 1024),
    )(activations, cotangent, conv_one, conv_two, bias_one.reshape(1, CH), bias_two.reshape(1, CH))
    taps = jnp.swapaxes(full[:, :9], 0, 1).reshape(3, 3, CH, 2 * CH)
    biases = jnp.sum(full[:, 9], axis=0)
    return symmetric_out, input_grad, taps[..., :CH], biases[:CH], taps[..., CH:], biases[CH:]


def solution(mesh):
    return jax.shard_map(
        on_device,
        mesh=mesh,
        in_specs=(P("row", "col"), P(), P(), P(), P(), P("row", "col")),
        out_specs=(P("row", "col"), P("row", "col"), P(), P(), P(), P()),
        check_vma=False,
    )
```

```python
import jax
import jax.numpy as jnp
from jax import lax
from jax.experimental import pallas as pl
from jax.experimental.pallas import tpu as pltpu
from jax.sharding import PartitionSpec as P

MESH = pl.DeviceIdType.MESH
F32 = jnp.float32
BF16 = jnp.bfloat16
CH = 64
ROWS = 32
WIDTH = 1024
QUAD = 256
INV_BINS = 1.0 / 512
PLANE = 32
DEPTH = 8
LINES = 10
SLOPE = 0.7978845608
CUBIC = 0.044715
AROUND = tuple((a, b) for a in (-1, 0, 1) for b in (-1, 0, 1) if a or b)
ENDS = {-1: (pl.ds(1, 1), pl.ds(5, 1)), 0: (pl.ds(1, 4), pl.ds(1, 4)), 1: (pl.ds(4, 1), pl.ds(0, 1))}
SIDES = {-1: (pl.ds(1, 1), pl.ds(3, 1)), 0: (pl.ds(1, 2), pl.ds(1, 2)), 1: (pl.ds(2, 1), pl.ds(0, 1))}


def plane_id(row, col, peer):
    return (lax.rem(peer, 2) * 8 + lax.rem(row, 8), (peer // 2) * 2 + lax.rem(col, 2))


def depth_id(row, col, peer):
    return ((row // 8) * 8 + peer, col)


def block_of(taps, transpose):
    zero = jnp.zeros((CH, CH), F32)
    value = taps.astype(F32)
    if transpose:
        value = value.T
    left = jnp.concatenate([value, zero], axis=1).astype(BF16)
    right = jnp.concatenate([zero, value], axis=1).astype(BF16)
    return left, right


def fill(matrix, taps_ref, flip):
    matrix[...] = jnp.zeros(matrix.shape, BF16)
    for a in range(3):
        for b in range(3):
            if flip:
                left, right = block_of(taps_ref[2 - a, 2 - b], True)
            else:
                left, right = block_of(taps_ref[a, b], False)
            for k in range(4):
                rows = pl.ds(b * QUAD + k * CH, CH)
                cols = pl.ds(a * QUAD + (k // 2) * 128, 128)
                matrix[rows, cols] = right if k % 2 else left


def pack(own, padded):
    for q in range(4):
        for g in range(2):
            rows = own[8 * q : 8 * q + 8]
            pair = [rows[:, QUAD * (2 * g + s) : QUAD * (2 * g + s + 1)] for s in range(2)]
            padded[q + 1, g + 1] = jnp.concatenate(pair, axis=0).astype(BF16)


def unpack(padded):
    values = padded[...].astype(F32)
    return [
        jnp.concatenate([values[q, g // 2, 8 * (g % 2) : 8 * (g % 2) + 8] for q in range(6)], axis=0).astype(BF16)
        for g in range(8)
    ]


def clear_edges(padded, row, col):
    @pl.when(row == 0)
    def _():
        padded[0] = jnp.zeros((4, 16, QUAD), BF16)

    @pl.when(row == 15)
    def _():
        padded[5] = jnp.zeros((4, 16, QUAD), BF16)

    @pl.when(col == 0)
    def _():
        padded[:, 0] = jnp.zeros((6, 16, QUAD), BF16)

    @pl.when(col == 31)
    def _():
        padded[:, 3] = jnp.zeros((6, 16, QUAD), BF16)


def conv(groups, matrix, rows):
    count = len(groups) - 2
    left = jnp.concatenate([jnp.stack(groups[b : b + count]) for b in range(3)], axis=-1)
    full = jnp.dot(left.reshape(count * 48, 3 * QUAD), matrix[...], preferred_element_type=F32)
    full = full.reshape(count, 48, 3 * QUAD)
    return (
        full[:, 0:rows, 0:QUAD]
        + full[:, 4 : 4 + rows, QUAD : 2 * QUAD]
        + full[:, 8 : 8 + rows, 2 * QUAD :]
    )


def taps_of(groups, grads):
    count, rows = grads.shape[:2]
    shifted = []
    for a in range(3):
        parts = [grads]
        if a:
            parts.insert(0, jnp.zeros((count, 4 * a, QUAD), F32))
        if 48 - rows - 4 * a:
            parts.append(jnp.zeros((count, 48 - rows - 4 * a, QUAD), F32))
        shifted.append(jnp.concatenate(parts, axis=1) if len(parts) > 1 else grads)
    right = jnp.concatenate(shifted, axis=-1).astype(BF16).reshape(count * 48, 3 * QUAD)
    out = []
    for b in range(3):
        left = jnp.stack(groups[b : b + count]).reshape(count * 48, QUAD)
        out.append(lax.dot_general(left, right, (((0,), (0,)), ((), ())), preferred_element_type=F32))
    return out


def halves(full, a):
    one = full[:, a * QUAD : a * QUAD + 128]
    two = full[:, a * QUAD + 128 : (a + 1) * QUAD]
    return one[0:64] + two[128:192], one[64:128] + two[192:256]


def turned(block, spare, base):
    lane = lax.broadcasted_iota(jnp.int32, (8, 128), 1)
    for p in range(8):
        spare[pl.ds(base + 16 * p, 16), :] = block[:, 128 * p : 128 * p + 128]
    for p in range(8):
        even = spare[pl.ds(base + 16 * p, 8, stride=2), :]
        odd = spare[pl.ds(base + 16 * p + 1, 8, stride=2), :]
        spare[pl.ds(base + 128 + 16 * p, 8), :] = jnp.where(lane < 64, even, pltpu.roll(odd, 64, 1))
        spare[pl.ds(base + 128 + 16 * p + 8, 8), :] = jnp.where(lane < 64, pltpu.roll(even, 64, 1), odd)
    return jnp.concatenate([spare[pl.ds(base + 128 + q, 16, stride=8), :] for q in range(8)], axis=1)


def grouped(tile):
    return jnp.stack([tile[:, QUAD * g : QUAD * (g + 1)] for g in range(4)])


def kernel(
    act_hbm, cot_hbm, one_hbm, two_hbm, bias_one_hbm, bias_two_hbm,
    sym_out, grad_out, full,
    act, cot, one, two, bias_one, bias_two, mat_one, mat_two, back_one, back_two,
    source_pad, sym_pad, mirror, summed, relay, mirror_sum, spare,
    parts, core_in, plane_in, depth_in,
    load_sem, m_send, m_recv, s_send, s_recv, r_send, r_recv, x_send, x_recv, g_send, g_recv, ar_send, ar_recv,
):
    row, col = lax.axis_index("row"), lax.axis_index("col")
    core = lax.rem(col, 2)
    plane = (col // 2) * 2 + row // 8
    depth = lax.rem(row, 8)
    sibling = (row, col + 1 - 2 * core)
    around = [(lax.rem(row + a + 16, 16), lax.rem(col + b + 32, 32)) for a, b in AROUND]
    opposite = [(col // 2, 2 * row + h) for h in range(2)]
    diagonal = col // 2 == row
    is_self = [diagonal & (core == h) for h in range(2)]

    barrier = pltpu.get_barrier_semaphore()
    for h in range(2):
        @pl.when(jnp.logical_not(is_self[h]))
        def _():
            pl.semaphore_signal(barrier, inc=1, device_id=opposite[h], device_id_type=MESH)
    for device in around + [sibling]:
        pl.semaphore_signal(barrier, inc=1, device_id=device, device_id_type=MESH)

    @pl.loop(1, PLANE)
    def _(step):
        pl.semaphore_signal(barrier, inc=1, device_id=plane_id(row, col, lax.rem(plane + step, PLANE)), device_id_type=MESH)

    @pl.loop(1, DEPTH)
    def _(step):
        pl.semaphore_signal(barrier, inc=1, device_id=depth_id(row, col, lax.rem(depth + step, DEPTH)), device_id_type=MESH)

    loads = [
        pltpu.make_async_copy(src, dst, load_sem.at[k])
        for k, (src, dst) in enumerate((
            (act_hbm, act), (one_hbm, one), (two_hbm, two), (cot_hbm, cot), (bias_one_hbm, bias_one), (bias_two_hbm, bias_two)
        ))
    ]
    for copy in loads:
        copy.start()
    loads[0].wait()
    source = act[...].astype(F32)
    pack(source, source_pad)

    def swap_start(src, dst, send, recv):
        for h in range(2):
            @pl.when(jnp.logical_not(is_self[h]))
            def _():
                pltpu.make_async_remote_copy(
                    src_ref=src.at[pl.ds(16 * h, 16)], dst_ref=dst.at[core], send_sem=send.at[h], recv_sem=recv.at[core],
                    device_id=opposite[h], device_id_type=MESH,
                ).start()

            @pl.when(is_self[h])
            def _():
                pltpu.make_async_copy(src.at[pl.ds(16 * h, 16)], dst.at[core], recv.at[core]).start()

    def swap_sent(src, dst, send):
        for h in range(2):
            @pl.when(jnp.logical_not(is_self[h]))
            def _():
                pltpu.make_async_copy(src.at[pl.ds(16 * h, 16)], dst.at[h], send.at[h]).wait()

    def halo_start(padded, send, recv):
        copies = []
        for k, (a, b) in enumerate(AROUND):
            copies.append(
                pltpu.make_async_remote_copy(
                    src_ref=padded.at[ENDS[a][0], SIDES[b][0]], dst_ref=padded.at[ENDS[a][1], SIDES[b][1]],
                    send_sem=send.at[k], recv_sem=recv.at[k], device_id=around[k], device_id_type=MESH,
                )
            )
            copies[-1].start()
        return copies

    pl.semaphore_wait(barrier, 2 + 8 + 1 + PLANE - 1 + DEPTH - 1 - diagonal.astype(jnp.int32))
    swap_start(cot_hbm, mirror, m_send, m_recv)
    source_halo = halo_start(source_pad, s_send, s_recv)

    for copy in loads[1:]:
        copy.wait()
    fill(mat_one, one, False)
    fill(mat_two, two, False)
    fill(back_two, two, True)
    fill(back_one, one, True)
    parts[8:CH, 9, :] = jnp.zeros((CH - 8, 128), F32)

    line = lax.broadcasted_iota(jnp.int32, (40, QUAD), 0)
    inside = ((line >= 4) | (row > 0)) & ((line < 36) | (row < 15))
    first = inside & (col > 0)
    last = inside & (col < 31)

    def masked(values):
        return jnp.stack([jnp.where((first, inside, inside, inside, inside, last)[g], values[g], 0.0) for g in range(6)])

    for copy in source_halo:
        copy.wait_recv()
    clear_edges(source_pad, row, col)
    source_groups = unpack(source_pad)
    wide_one = jnp.concatenate([bias_one[...]] * 4, axis=1)
    wide_two = jnp.concatenate([bias_two[...]] * 4, axis=1)
    preact = conv(source_groups, mat_one, 40) + wide_one
    bent = jnp.tanh(SLOPE * (preact + CUBIC * preact * preact * preact))
    hidden = masked(0.5 * preact * (1.0 + bent))
    slope = masked(
        0.5 * (1.0 + bent)
        + 0.5 * preact * (1.0 - bent * bent) * (SLOPE * (1.0 + 3.0 * CUBIC * preact * preact))
    )
    blank = jnp.zeros((6, 8, QUAD), F32)
    hidden = jnp.concatenate([hidden, blank], axis=1).astype(BF16)
    hidden_groups = [hidden[g] for g in range(6)]
    branch = conv(hidden_groups, mat_two, 32) + wide_two
    summed[...] = (source + jnp.concatenate([branch[g] for g in range(4)], axis=1)).astype(BF16)

    for step in range(1, DEPTH):
        pltpu.make_async_remote_copy(
            src_ref=summed.at[:, pl.ds(128 * step, 128)], dst_ref=relay.at[depth], send_sem=r_send, recv_sem=r_recv,
            device_id=depth_id(row, col, lax.rem(depth + step, DEPTH)), device_id_type=MESH,
        ).start()
    relay[depth] = summed[:, 0:128]
    for h in range(2):
        pltpu.make_async_copy(mirror.at[h], mirror.at[h], m_recv.at[h]).wait()
    turned_cot = jnp.concatenate([turned(mirror[h].astype(F32), spare, 256 * h) for h in range(2)], axis=0)
    sym = ((cot[...].astype(F32) + turned_cot) * 0.5).astype(BF16).astype(F32)
    pack(sym, sym_pad)
    sym_halo = halo_start(sym_pad, g_send, g_recv)

    sym_own = grouped(sym)
    lower = jnp.zeros((4, 8, QUAD), F32)
    sym_rows = jnp.concatenate([lower, sym_own, lower], axis=1).astype(BF16)
    nothing = jnp.zeros((48, QUAD), BF16)
    sym_groups = [nothing] * 2 + [sym_rows[g] for g in range(4)] + [nothing] * 2
    share = conv(sym_groups, back_two, 40) * slope
    taps_two = taps_of(hidden_groups, sym_own)
    taps_one = taps_of(source_groups, share)
    left = lax.broadcasted_iota(jnp.int32, (CH, 128), 1) < CH
    for a in range(3):
        for b in range(3):
            near_one, far_one = halves(taps_one[b], a)
            near_two, far_two = halves(taps_two[b], a)
            parts[:, 3 * a + b, :] = jnp.where(
                left, near_one + pltpu.roll(far_one, CH, 1), far_two + pltpu.roll(near_two, CH, 1)
            )
    bias = []
    for grads in (share, sym_own):
        total = jnp.sum(grads.reshape(-1, 8, QUAD), axis=0)
        total = total[:, :128] + total[:, 128:]
        bias.append(total + pltpu.roll(total, CH, 1))
    parts[0:8, 9, :] = jnp.where(left[:8], bias[0], bias[1])

    own = pl.ds(PLANE * core, PLANE)
    to_core = pltpu.make_async_remote_copy(
        src_ref=parts.at[pl.ds(PLANE * (1 - core), PLANE)], dst_ref=core_in, send_sem=ar_send.at[0], recv_sem=ar_recv.at[0],
        device_id=sibling, device_id_type=MESH,
    )
    to_core.start()
    to_core.wait_recv()
    core_in[...] = core_in[...] + parts[own]

    @pl.loop(1, PLANE)
    def _(step):
        peer = lax.rem(plane + step, PLANE)
        pltpu.make_async_remote_copy(
            src_ref=core_in.at[peer], dst_ref=plane_in.at[step - 1], send_sem=ar_send.at[1], recv_sem=ar_recv.at[1],
            device_id=plane_id(row, col, peer), device_id_type=MESH,
        ).start()

    pltpu.make_async_copy(relay.at[pl.ds(0, DEPTH - 1)], relay.at[pl.ds(0, DEPTH - 1)], r_recv).wait()

    @pl.loop(0, DEPTH)
    def _(origin):
        lanes = pl.ds(pl.multiple_of(128 * lax.rem(depth - origin + DEPTH, DEPTH), 128), 128)
        for h in range(2):
            src, dst = relay.at[origin, pl.ds(16 * h, 16)], mirror_sum.at[core, :, lanes]
            here = is_self[h] & (origin == depth)

            @pl.when(jnp.logical_not(here))
            def _():
                pltpu.make_async_remote_copy(
                    src_ref=src, dst_ref=dst, send_sem=x_send, recv_sem=x_recv,
                    device_id=(col // 2, 2 * (row - depth + origin) + h), device_id_type=MESH,
                ).start()

            @pl.when(here)
            def _():
                pltpu.make_async_copy(src, dst, x_recv).start()

    for copy in sym_halo:
        copy.wait_recv()
    clear_edges(sym_pad, row, col)
    pre_grad = conv(unpack(sym_pad), back_two, 40) * slope
    pre_grad = jnp.concatenate([pre_grad, blank], axis=1).astype(BF16)
    input_grad = conv([pre_grad[g] for g in range(6)], back_one, 32)
    grad_out[...] = (sym + jnp.concatenate([input_grad[g] for g in range(4)], axis=1)).astype(BF16)

    pltpu.make_async_copy(plane_in, plane_in, ar_recv.at[1]).wait()
    depth_in[depth] = jnp.sum(plane_in[...], axis=0) + core_in[plane]

    @pl.loop(1, DEPTH)
    def _(step):
        peer = lax.rem(depth + step, DEPTH)
        pltpu.make_async_remote_copy(
            src_ref=depth_in.at[depth], dst_ref=depth_in.at[depth], send_sem=ar_send.at[2], recv_sem=ar_recv.at[2],
            device_id=depth_id(row, col, peer), device_id_type=MESH,
        ).start()

    pltpu.make_async_copy(depth_in.at[pl.ds(0, DEPTH - 1)], depth_in.at[pl.ds(0, DEPTH - 1)], ar_recv.at[2]).wait()
    here = PLANE * core + plane
    full[here] = jnp.sum(depth_in[...], axis=0) * INV_BINS

    @pl.loop(1, PLANE)
    def _(step):
        pltpu.make_async_remote_copy(
            src_ref=full.at[here], dst_ref=full.at[here], send_sem=ar_send.at[3], recv_sem=ar_recv.at[3],
            device_id=plane_id(row, col, lax.rem(plane + step, PLANE)), device_id_type=MESH,
        ).start()

    pltpu.make_async_copy(plane_in, plane_in, ar_recv.at[3]).wait()
    back_core = pltpu.make_async_remote_copy(
        src_ref=full.at[own], dst_ref=full.at[own], send_sem=ar_send.at[4], recv_sem=ar_recv.at[4],
        device_id=sibling, device_id_type=MESH,
    )
    back_core.start()
    pltpu.make_async_copy(mirror_sum, mirror_sum, x_recv).wait()
    turned_sum = jnp.concatenate([turned(mirror_sum[h].astype(F32), spare, 256 * h) for h in range(2)], axis=0)
    sym_out[...] = ((summed[...].astype(F32) + turned_sum) * 0.5).astype(BF16)

    swap_sent(cot_hbm, mirror, m_send)
    pltpu.make_async_copy(relay.at[pl.ds(0, DEPTH - 1)], relay.at[pl.ds(0, DEPTH - 1)], r_send).wait()

    @pl.when(jnp.logical_not(diagonal))
    def _():
        pltpu.make_async_copy(mirror_sum, mirror_sum, x_send).wait()

    @pl.when(diagonal)
    def _():
        piece = mirror_sum.at[0, :, pl.ds(0, 7 * 128)]
        pltpu.make_async_copy(mirror_sum.at[1], mirror_sum.at[1], x_send).wait()
        pltpu.make_async_copy(piece, piece, x_send).wait()

    for copy in source_halo + sym_halo + [to_core]:
        copy.wait_send()
    pltpu.make_async_copy(plane_in, plane_in, ar_send.at[1]).wait()
    pltpu.make_async_copy(depth_in.at[pl.ds(0, DEPTH - 1)], depth_in.at[pl.ds(0, DEPTH - 1)], ar_send.at[2]).wait()
    pltpu.make_async_copy(plane_in, plane_in, ar_send.at[3]).wait()
    back_core.wait()


def unfold(sym, grad, full, sym_out, grad_out, one_out, bias_one_out, two_out, bias_two_out, sems):
    copies = [pltpu.make_async_copy(sym, sym_out, sems.at[0]), pltpu.make_async_copy(grad, grad_out, sems.at[1])]
    for copy in copies:
        copy.start()
    for a in range(3):
        for b in range(3):
            tap = full[:, 3 * a + b, :]
            one_out[a, b] = tap[:, :CH]
            two_out[a, b] = pltpu.roll(tap, CH, 1)[:, :CH]
    bias = jnp.sum(full[:, 9, :], axis=0, keepdims=True)
    bias_one_out[...] = bias[:, :CH]
    bias_two_out[...] = pltpu.roll(bias, CH, 1)[:, :CH]
    for copy in copies:
        copy.wait()


def on_device(activations, conv_one, bias_one, conv_two, bias_two, cotangent):
    vmem, anywhere = pl.BlockSpec(memory_space=pltpu.VMEM), pl.BlockSpec(memory_space=pl.ANY)
    dma = pltpu.SemaphoreType.DMA
    tile = jax.ShapeDtypeStruct((ROWS, WIDTH), BF16)
    inputs = (activations, cotangent, conv_one, conv_two, bias_one.reshape(1, CH), bias_two.reshape(1, CH))
    held = pl.pallas_call(
        kernel,
        out_shape=(
            pltpu.VMEM((ROWS, WIDTH), BF16),
            pltpu.VMEM((ROWS, WIDTH), BF16),
            pltpu.VMEM((CH, LINES, 128), F32),
        ),
        in_specs=[anywhere] * 6,
        out_specs=[vmem] * 3,
        scratch_shapes=[
            pltpu.VMEM((ROWS, WIDTH), BF16),
            pltpu.VMEM((ROWS, WIDTH), BF16),
            pltpu.VMEM((3, 3, CH, CH), BF16),
            pltpu.VMEM((3, 3, CH, CH), BF16),
            pltpu.VMEM((1, CH), F32),
            pltpu.VMEM((1, CH), F32),
        ]
        + [pltpu.VMEM((3 * QUAD, 3 * QUAD), BF16)] * 4
        + [
            pltpu.VMEM((6, 4, 16, QUAD), BF16),
            pltpu.VMEM((6, 4, 16, QUAD), BF16),
            pltpu.VMEM((2, 16, WIDTH), BF16),
            pltpu.VMEM((ROWS, WIDTH), BF16),
            pltpu.VMEM((DEPTH, ROWS, 128), BF16),
            pltpu.VMEM((2, 16, WIDTH), BF16),
            pltpu.VMEM((512, 128), F32),
            pltpu.VMEM((CH, LINES, 128), F32),
            pltpu.VMEM((PLANE, LINES, 128), F32),
            pltpu.VMEM((PLANE - 1, LINES, 128), F32),
            pltpu.VMEM((DEPTH, LINES, 128), F32),
            dma((6,)), dma((2,)), dma((2,)), dma((8,)), dma((8,)), dma, dma, dma, dma, dma((8,)), dma((8,)), dma((5,)), dma((5,)),
        ],
        compiler_params=pltpu.CompilerParams(collective_id=0, has_side_effects=True, vmem_limit_bytes=48 * 1024 * 1024),
    )(*(pltpu.with_memory_space_constraint(x, pltpu.HBM) for x in inputs))
    taps = jax.ShapeDtypeStruct((3, 3, CH, CH), F32)
    bias = jax.ShapeDtypeStruct((1, CH), F32)
    symmetric_out, input_grad, grad_w1, grad_b1, grad_w2, grad_b2 = pl.pallas_call(
        unfold,
        out_shape=(tile, tile, taps, bias, taps, bias),
        in_specs=[vmem] * 3,
        out_specs=[anywhere] * 2 + [vmem] * 4,
        scratch_shapes=[dma((2,))],
        compiler_params=pltpu.CompilerParams(vmem_limit_bytes=8 * 1024 * 1024),
    )(*(pltpu.with_memory_space_constraint(x, pltpu.VMEM) for x in held))
    return symmetric_out, input_grad, grad_w1, grad_b1.reshape(CH), grad_w2, grad_b2.reshape(CH)


def solution(mesh):
    return jax.shard_map(
        on_device,
        mesh=mesh,
        in_specs=(P("row", "col"), P(), P(), P(), P(), P("row", "col")),
        out_specs=(P("row", "col"), P("row", "col"), P(), P(), P(), P()),
        check_vma=False,
    )
```

```python
import jax
import jax.numpy as jnp
from jax import lax
from jax.experimental import pallas as pl
from jax.experimental.pallas import tpu as pltpu
from jax.sharding import PartitionSpec as P

MESH = pl.DeviceIdType.MESH
F32 = jnp.float32
BF16 = jnp.bfloat16
CH = 64
ROWS = 32
WIDTH = 1024
QUAD = 256
INV_BINS = 1.0 / 512
PLANE = 32
DEPTH = 8
LINES = 10
SLOPE = 0.7978845608
CUBIC = 0.044715
AROUND = tuple((a, b) for a in (-1, 0, 1) for b in (-1, 0, 1) if a or b)
ENDS = {-1: (pl.ds(1, 1), pl.ds(5, 1)), 0: (pl.ds(1, 4), pl.ds(1, 4)), 1: (pl.ds(4, 1), pl.ds(0, 1))}
SIDES = {-1: (pl.ds(1, 1), pl.ds(3, 1)), 0: (pl.ds(1, 2), pl.ds(1, 2)), 1: (pl.ds(2, 1), pl.ds(0, 1))}


def plane_id(row, col, peer):
    return (lax.rem(peer, 2) * 8 + lax.rem(row, 8), (peer // 2) * 2 + lax.rem(col, 2))


def depth_id(row, col, peer):
    return ((row // 8) * 8 + peer, col)


def block_of(taps, transpose):
    zero = jnp.zeros((CH, CH), F32)
    value = taps.astype(F32)
    if transpose:
        value = value.T
    left = jnp.concatenate([value, zero], axis=1).astype(BF16)
    right = jnp.concatenate([zero, value], axis=1).astype(BF16)
    return left, right


def fill(matrix, taps_ref, flip):
    matrix[...] = jnp.zeros(matrix.shape, BF16)
    for a in range(3):
        for b in range(3):
            if flip:
                left, right = block_of(taps_ref[2 - a, 2 - b], True)
            else:
                left, right = block_of(taps_ref[a, b], False)
            for k in range(4):
                rows = pl.ds(b * QUAD + k * CH, CH)
                cols = pl.ds(a * QUAD + (k // 2) * 128, 128)
                matrix[rows, cols] = right if k % 2 else left


def pack(own, padded):
    for q in range(4):
        for g in range(2):
            rows = own[8 * q : 8 * q + 8]
            pair = [rows[:, QUAD * (2 * g + s) : QUAD * (2 * g + s + 1)] for s in range(2)]
            padded[q + 1, g + 1] = jnp.concatenate(pair, axis=0).astype(BF16)


def unpack(padded):
    values = padded[...].astype(F32)
    return [
        jnp.concatenate([values[q, g // 2, 8 * (g % 2) : 8 * (g % 2) + 8] for q in range(6)], axis=0)
        for g in range(8)
    ]


def clear_edges(padded, row, col):
    @pl.when(row == 0)
    def _():
        padded[0] = jnp.zeros((4, 16, QUAD), BF16)

    @pl.when(row == 15)
    def _():
        padded[5] = jnp.zeros((4, 16, QUAD), BF16)

    @pl.when(col == 0)
    def _():
        padded[:, 0] = jnp.zeros((6, 16, QUAD), BF16)

    @pl.when(col == 31)
    def _():
        padded[:, 3] = jnp.zeros((6, 16, QUAD), BF16)


def conv(groups, matrix, rows):
    count = len(groups) - 2
    groups = [group.astype(BF16) for group in groups]
    left = jnp.concatenate([jnp.stack(groups[b : b + count]) for b in range(3)], axis=-1)
    full = jnp.dot(left.reshape(count * 48, 3 * QUAD), matrix[...], preferred_element_type=F32)
    full = full.reshape(count, 48, 3 * QUAD)
    return (
        full[:, 0:rows, 0:QUAD]
        + full[:, 4 : 4 + rows, QUAD : 2 * QUAD]
        + full[:, 8 : 8 + rows, 2 * QUAD :]
    )


def spread(own, matrix):
    left = own.reshape(128, QUAD).astype(BF16)
    columns = []
    for b in range(3):
        full = jnp.dot(left, matrix[b * QUAD : (b + 1) * QUAD], preferred_element_type=F32).reshape(4, 32, 3 * QUAD)
        lower, upper = jnp.zeros((4, 4, QUAD), F32), jnp.zeros((4, 8, QUAD), F32)
        columns.append(
            jnp.concatenate([upper, full[:, :, :QUAD]], axis=1)
            + jnp.concatenate([lower, full[:, :, QUAD : 2 * QUAD], lower], axis=1)
            + jnp.concatenate([full[:, :, 2 * QUAD :], upper], axis=1)
        )
    out = []
    for g in range(6):
        terms = [columns[b][g - 2 + b] for b in range(3) if 0 <= g - 2 + b < 4]
        out.append(sum(terms[1:], terms[0]))
    return jnp.stack(out)


def windows(groups, count, rows, turned_rows):
    for a in range(3):
        for b in range(3):
            window = jnp.concatenate([groups[g][4 * a : 4 * a + rows] for g in range(b, b + count)], axis=0)
            turned_rows[pl.ds(QUAD * (3 * a + b), QUAD), 0 : count * rows] = window.astype(BF16).T


def halves(full, tap):
    one = full[tap * QUAD : (tap + 1) * QUAD, :128]
    two = full[tap * QUAD : (tap + 1) * QUAD, 128:]
    return one[0:64] + two[128:192], one[64:128] + two[192:256]


def turned(block, spare, base):
    lane = lax.broadcasted_iota(jnp.int32, (8, 128), 1)
    for p in range(8):
        spare[pl.ds(base + 16 * p, 16), :] = block[:, 128 * p : 128 * p + 128]
    for p in range(8):
        even = spare[pl.ds(base + 16 * p, 8, stride=2), :]
        odd = spare[pl.ds(base + 16 * p + 1, 8, stride=2), :]
        spare[pl.ds(base + 128 + 16 * p, 8), :] = jnp.where(lane < 64, even, pltpu.roll(odd, 64, 1))
        spare[pl.ds(base + 128 + 16 * p + 8, 8), :] = jnp.where(lane < 64, pltpu.roll(even, 64, 1), odd)
    return jnp.concatenate([spare[pl.ds(base + 128 + q, 16, stride=8), :] for q in range(8)], axis=1)


def grouped(tile):
    return jnp.stack([tile[:, QUAD * g : QUAD * (g + 1)] for g in range(4)])


def kernel(
    act_hbm, cot_hbm, one_hbm, two_hbm, bias_one_hbm, bias_two_hbm,
    sym_out, grad_out, full,
    act, cot, one, two, bias_one, bias_two, mat_one, mat_two, back_one, back_two,
    source_pad, sym_pad, mirror, summed, relay, mirror_sum, spare,
    hidden_turned, source_turned, parts, core_in, plane_in, depth_in,
    load_sem, m_send, m_recv, s_send, s_recv, r_send, r_recv, x_send, x_recv, g_send, g_recv, ar_send, ar_recv,
):
    row, col = lax.axis_index("row"), lax.axis_index("col")
    core = lax.rem(col, 2)
    plane = (col // 2) * 2 + row // 8
    depth = lax.rem(row, 8)
    sibling = (row, col + 1 - 2 * core)
    around = [(lax.rem(row + a + 16, 16), lax.rem(col + b + 32, 32)) for a, b in AROUND]
    opposite = [(col // 2, 2 * row + h) for h in range(2)]
    diagonal = col // 2 == row
    is_self = [diagonal & (core == h) for h in range(2)]

    loads = [
        pltpu.make_async_copy(src, dst, load_sem.at[k])
        for k, (src, dst) in enumerate((
            (act_hbm, act), (one_hbm, one), (two_hbm, two), (cot_hbm, cot), (bias_one_hbm, bias_one), (bias_two_hbm, bias_two)
        ))
    ]
    for copy in loads:
        copy.start()
    barrier = pltpu.get_barrier_semaphore()
    for h in range(2):
        @pl.when(jnp.logical_not(is_self[h]))
        def _():
            pl.semaphore_signal(barrier, inc=1, device_id=opposite[h], device_id_type=MESH)
    for device in around + [sibling]:
        pl.semaphore_signal(barrier, inc=1, device_id=device, device_id_type=MESH)

    @pl.loop(1, PLANE)
    def _(step):
        pl.semaphore_signal(barrier, inc=1, device_id=plane_id(row, col, lax.rem(plane + step, PLANE)), device_id_type=MESH)

    @pl.loop(1, DEPTH)
    def _(step):
        pl.semaphore_signal(barrier, inc=1, device_id=depth_id(row, col, lax.rem(depth + step, DEPTH)), device_id_type=MESH)

    loads[0].wait()
    source = act[...].astype(F32)
    pack(source, source_pad)

    def swap_start(src, dst, send, recv):
        for h in range(2):
            @pl.when(jnp.logical_not(is_self[h]))
            def _():
                pltpu.make_async_remote_copy(
                    src_ref=src.at[pl.ds(16 * h, 16)], dst_ref=dst.at[core], send_sem=send.at[h], recv_sem=recv.at[core],
                    device_id=opposite[h], device_id_type=MESH,
                ).start()

            @pl.when(is_self[h])
            def _():
                pltpu.make_async_copy(src.at[pl.ds(16 * h, 16)], dst.at[core], recv.at[core]).start()

    def swap_sent(src, dst, send):
        for h in range(2):
            @pl.when(jnp.logical_not(is_self[h]))
            def _():
                pltpu.make_async_copy(src.at[pl.ds(16 * h, 16)], dst.at[h], send.at[h]).wait()

    def halo_start(padded, send, recv):
        copies = []
        for k, (a, b) in enumerate(AROUND):
            copies.append(
                pltpu.make_async_remote_copy(
                    src_ref=padded.at[ENDS[a][0], SIDES[b][0]], dst_ref=padded.at[ENDS[a][1], SIDES[b][1]],
                    send_sem=send.at[k], recv_sem=recv.at[k], device_id=around[k], device_id_type=MESH,
                )
            )
            copies[-1].start()
        return copies

    loads[3].wait()
    pl.semaphore_wait(barrier, 2 + 8 + 1 + PLANE - 1 + DEPTH - 1 - diagonal.astype(jnp.int32))
    swap_start(cot, mirror, m_send, m_recv)
    source_halo = halo_start(source_pad, s_send, s_recv)

    for k in (1, 2, 4, 5):
        loads[k].wait()
    fill(mat_one, one, False)
    fill(mat_two, two, False)
    fill(back_two, two, True)
    fill(back_one, one, True)
    parts[8:CH, 9, :] = jnp.zeros((CH - 8, 128), F32)

    line = lax.broadcasted_iota(jnp.int32, (40, QUAD), 0)
    inside = ((line >= 4) | (row > 0)) & ((line < 36) | (row < 15))
    first = inside & (col > 0)
    last = inside & (col < 31)

    def masked(values):
        return jnp.stack([jnp.where((first, inside, inside, inside, inside, last)[g], values[g], 0.0) for g in range(6)])

    for copy in source_halo:
        copy.wait_recv()
    clear_edges(source_pad, row, col)
    source_groups = unpack(source_pad)
    wide_one = jnp.concatenate([bias_one[...]] * 4, axis=1)
    wide_two = jnp.concatenate([bias_two[...]] * 4, axis=1)
    preact = conv(source_groups, mat_one, 40) + wide_one
    bent = jnp.tanh(SLOPE * (preact + CUBIC * preact * preact * preact))
    hidden = masked(0.5 * preact * (1.0 + bent))
    slope = masked(
        0.5 * (1.0 + bent)
        + 0.5 * preact * (1.0 - bent * bent) * (SLOPE * (1.0 + 3.0 * CUBIC * preact * preact))
    )
    blank = jnp.zeros((6, 8, QUAD), F32)
    hidden = jnp.concatenate([hidden, blank], axis=1)
    hidden_groups = [hidden[g] for g in range(6)]
    branch = conv(hidden_groups, mat_two, 32) + wide_two
    summed[...] = (source + jnp.concatenate([branch[g] for g in range(4)], axis=1)).astype(BF16)

    for step in range(1, DEPTH):
        pltpu.make_async_remote_copy(
            src_ref=summed.at[:, pl.ds(128 * step, 128)], dst_ref=relay.at[depth], send_sem=r_send, recv_sem=r_recv,
            device_id=depth_id(row, col, lax.rem(depth + step, DEPTH)), device_id_type=MESH,
        ).start()
    relay[depth] = summed[:, 0:128]
    windows(hidden_groups, 4, 32, hidden_turned)
    windows(source_groups, 6, 40, source_turned)
    source_turned[:, 240:QUAD] = jnp.zeros((9 * QUAD, 16), BF16)
    for h in range(2):
        pltpu.make_async_copy(mirror.at[h], mirror.at[h], m_recv.at[h]).wait()
    turned_cot = jnp.concatenate([turned(mirror[h].astype(F32), spare, 256 * h) for h in range(2)], axis=0)
    sym = ((cot[...].astype(F32) + turned_cot) * 0.5).astype(BF16).astype(F32)

    sym_own = grouped(sym)
    share = spread(sym_own, back_two) * slope
    taps_two = jnp.dot(hidden_turned[...], sym_own.reshape(128, QUAD).astype(BF16), preferred_element_type=F32)
    rows = jnp.concatenate([share.reshape(240, QUAD), jnp.zeros((16, QUAD), F32)], axis=0).astype(BF16)
    taps_one = jnp.dot(source_turned[...], rows, preferred_element_type=F32)
    left = lax.broadcasted_iota(jnp.int32, (CH, 128), 1) < CH
    for a in range(3):
        for b in range(3):
            near_one, far_one = halves(taps_one, 3 * a + b)
            near_two, far_two = halves(taps_two, 3 * a + b)
            parts[:, 3 * a + b, :] = jnp.where(
                left, near_one + pltpu.roll(far_one, CH, 1), far_two + pltpu.roll(near_two, CH, 1)
            )
    bias = []
    for grads in (share, sym_own):
        total = jnp.sum(grads.reshape(-1, 8, QUAD), axis=0)
        total = total[:, :128] + total[:, 128:]
        bias.append(total + pltpu.roll(total, CH, 1))
    parts[0:8, 9, :] = jnp.where(left[:8], bias[0], bias[1])

    own = pl.ds(PLANE * core, PLANE)
    to_core = pltpu.make_async_remote_copy(
        src_ref=parts.at[pl.ds(PLANE * (1 - core), PLANE)], dst_ref=core_in, send_sem=ar_send.at[0], recv_sem=ar_recv.at[0],
        device_id=sibling, device_id_type=MESH,
    )
    to_core.start()
    pack(sym, sym_pad)
    sym_halo = halo_start(sym_pad, g_send, g_recv)
    to_core.wait_recv()
    core_in[...] = core_in[...] + parts[own]

    @pl.loop(1, PLANE)
    def _(step):
        peer = lax.rem(plane + step, PLANE)
        pltpu.make_async_remote_copy(
            src_ref=core_in.at[peer], dst_ref=plane_in.at[step - 1], send_sem=ar_send.at[1], recv_sem=ar_recv.at[1],
            device_id=plane_id(row, col, peer), device_id_type=MESH,
        ).start()

    pltpu.make_async_copy(relay.at[pl.ds(0, DEPTH - 1)], relay.at[pl.ds(0, DEPTH - 1)], r_recv).wait()

    @pl.loop(0, DEPTH)
    def _(origin):
        lanes = pl.ds(pl.multiple_of(128 * lax.rem(depth - origin + DEPTH, DEPTH), 128), 128)
        for h in range(2):
            src, dst = relay.at[origin, pl.ds(16 * h, 16)], mirror_sum.at[core, :, lanes]
            here = is_self[h] & (origin == depth)

            @pl.when(jnp.logical_not(here))
            def _():
                pltpu.make_async_remote_copy(
                    src_ref=src, dst_ref=dst, send_sem=x_send, recv_sem=x_recv,
                    device_id=(col // 2, 2 * (row - depth + origin) + h), device_id_type=MESH,
                ).start()

            @pl.when(here)
            def _():
                pltpu.make_async_copy(src, dst, x_recv).start()

    pltpu.make_async_copy(plane_in, plane_in, ar_recv.at[1]).wait()
    depth_in[depth] = jnp.sum(plane_in[...], axis=0) + core_in[plane]

    @pl.loop(1, DEPTH)
    def _(step):
        peer = lax.rem(depth + step, DEPTH)
        pltpu.make_async_remote_copy(
            src_ref=depth_in.at[depth], dst_ref=depth_in.at[depth], send_sem=ar_send.at[2], recv_sem=ar_recv.at[2],
            device_id=depth_id(row, col, peer), device_id_type=MESH,
        ).start()

    pltpu.make_async_copy(depth_in.at[pl.ds(0, DEPTH - 1)], depth_in.at[pl.ds(0, DEPTH - 1)], ar_recv.at[2]).wait()
    here = PLANE * core + plane
    full[here] = jnp.sum(depth_in[...], axis=0) * INV_BINS

    @pl.loop(1, PLANE)
    def _(step):
        pltpu.make_async_remote_copy(
            src_ref=full.at[here], dst_ref=full.at[here], send_sem=ar_send.at[3], recv_sem=ar_recv.at[3],
            device_id=plane_id(row, col, lax.rem(plane + step, PLANE)), device_id_type=MESH,
        ).start()

    for copy in sym_halo:
        copy.wait_recv()
    clear_edges(sym_pad, row, col)
    pre_grad = conv(unpack(sym_pad), back_two, 40) * slope
    pre_grad = jnp.concatenate([pre_grad, blank], axis=1).astype(BF16)
    input_grad = conv([pre_grad[g] for g in range(6)], back_one, 32)
    grad_out[...] = (sym + jnp.concatenate([input_grad[g] for g in range(4)], axis=1)).astype(BF16)

    pltpu.make_async_copy(plane_in, plane_in, ar_recv.at[3]).wait()
    back_core = pltpu.make_async_remote_copy(
        src_ref=full.at[own], dst_ref=full.at[own], send_sem=ar_send.at[4], recv_sem=ar_recv.at[4],
        device_id=sibling, device_id_type=MESH,
    )
    back_core.start()
    pltpu.make_async_copy(mirror_sum, mirror_sum, x_recv).wait()
    turned_sum = jnp.concatenate([turned(mirror_sum[h].astype(F32), spare, 256 * h) for h in range(2)], axis=0)
    sym_out[...] = ((summed[...].astype(F32) + turned_sum) * 0.5).astype(BF16)

    swap_sent(cot, mirror, m_send)
    pltpu.make_async_copy(relay.at[pl.ds(0, DEPTH - 1)], relay.at[pl.ds(0, DEPTH - 1)], r_send).wait()

    @pl.when(jnp.logical_not(diagonal))
    def _():
        pltpu.make_async_copy(mirror_sum, mirror_sum, x_send).wait()

    @pl.when(diagonal)
    def _():
        piece = mirror_sum.at[0, :, pl.ds(0, 7 * 128)]
        pltpu.make_async_copy(mirror_sum.at[1], mirror_sum.at[1], x_send).wait()
        pltpu.make_async_copy(piece, piece, x_send).wait()

    for copy in source_halo + sym_halo + [to_core]:
        copy.wait_send()
    pltpu.make_async_copy(plane_in, plane_in, ar_send.at[1]).wait()
    pltpu.make_async_copy(depth_in.at[pl.ds(0, DEPTH - 1)], depth_in.at[pl.ds(0, DEPTH - 1)], ar_send.at[2]).wait()
    pltpu.make_async_copy(plane_in, plane_in, ar_send.at[3]).wait()
    back_core.wait()


def unfold(sym, grad, full, sym_out, grad_out, one_out, bias_one_out, two_out, bias_two_out, one, two, bias_one, bias_two, sems):
    def send(k, src, dst):
        copy = pltpu.make_async_copy(src, dst, sems.at[k])
        copy.start()
        return copy

    copies = [send(0, sym, sym_out), send(1, grad, grad_out)]
    bias = jnp.sum(full[:, 9, :], axis=0, keepdims=True)
    bias_one[...] = bias[:, :CH]
    bias_two[...] = pltpu.roll(bias, CH, 1)[:, :CH]
    copies += [send(2, bias_one, bias_one_out), send(3, bias_two, bias_two_out)]
    for a in range(3):
        for b in range(3):
            tap = full[:, 3 * a + b, :]
            one[a, b] = tap[:, :CH]
            two[a, b] = pltpu.roll(tap, CH, 1)[:, :CH]
        copies += [send(4 + a, one.at[a], one_out.at[a]), send(7 + a, two.at[a], two_out.at[a])]
    for copy in copies:
        copy.wait()


def on_device(activations, conv_one, bias_one, conv_two, bias_two, cotangent):
    vmem, anywhere = pl.BlockSpec(memory_space=pltpu.VMEM), pl.BlockSpec(memory_space=pl.ANY)
    dma = pltpu.SemaphoreType.DMA
    tile = jax.ShapeDtypeStruct((ROWS, WIDTH), BF16)
    inputs = (activations, cotangent, conv_one, conv_two, bias_one.reshape(1, CH), bias_two.reshape(1, CH))
    held = pl.pallas_call(
        kernel,
        out_shape=(
            pltpu.VMEM((ROWS, WIDTH), BF16),
            pltpu.VMEM((ROWS, WIDTH), BF16),
            pltpu.VMEM((CH, LINES, 128), F32),
        ),
        in_specs=[anywhere] * 6,
        out_specs=[vmem] * 3,
        scratch_shapes=[
            pltpu.VMEM((ROWS, WIDTH), BF16),
            pltpu.VMEM((ROWS, WIDTH), BF16),
            pltpu.VMEM((3, 3, CH, CH), BF16),
            pltpu.VMEM((3, 3, CH, CH), BF16),
            pltpu.VMEM((1, CH), F32),
            pltpu.VMEM((1, CH), F32),
        ]
        + [pltpu.VMEM((3 * QUAD, 3 * QUAD), BF16)] * 4
        + [
            pltpu.VMEM((6, 4, 16, QUAD), BF16),
            pltpu.VMEM((6, 4, 16, QUAD), BF16),
            pltpu.VMEM((2, 16, WIDTH), BF16),
            pltpu.VMEM((ROWS, WIDTH), BF16),
            pltpu.VMEM((DEPTH, ROWS, 128), BF16),
            pltpu.VMEM((2, 16, WIDTH), BF16),
            pltpu.VMEM((512, 128), F32),
            pltpu.VMEM((9 * QUAD, 128), BF16),
            pltpu.VMEM((9 * QUAD, QUAD), BF16),
            pltpu.VMEM((CH, LINES, 128), F32),
            pltpu.VMEM((PLANE, LINES, 128), F32),
            pltpu.VMEM((PLANE - 1, LINES, 128), F32),
            pltpu.VMEM((DEPTH, LINES, 128), F32),
            dma((6,)), dma((2,)), dma((2,)), dma((8,)), dma((8,)), dma, dma, dma, dma, dma((8,)), dma((8,)), dma((5,)), dma((5,)),
        ],
        compiler_params=pltpu.CompilerParams(collective_id=0, has_side_effects=True, vmem_limit_bytes=48 * 1024 * 1024),
    )(*(pltpu.with_memory_space_constraint(x, pltpu.HBM) for x in inputs))
    taps = jax.ShapeDtypeStruct((3, 3, CH, CH), F32)
    bias = jax.ShapeDtypeStruct((1, CH), F32)
    symmetric_out, input_grad, grad_w1, grad_b1, grad_w2, grad_b2 = pl.pallas_call(
        unfold,
        out_shape=(tile, tile, taps, bias, taps, bias),
        in_specs=[vmem] * 3,
        out_specs=[anywhere] * 6,
        scratch_shapes=[pltpu.VMEM((3, 3, CH, CH), F32)] * 2 + [pltpu.VMEM((1, CH), F32)] * 2 + [dma((10,))],
        compiler_params=pltpu.CompilerParams(vmem_limit_bytes=8 * 1024 * 1024),
    )(*(pltpu.with_memory_space_constraint(x, pltpu.VMEM) for x in held))
    return symmetric_out, input_grad, grad_w1, grad_b1.reshape(CH), grad_w2, grad_b2.reshape(CH)


def solution(mesh):
    return jax.shard_map(
        on_device,
        mesh=mesh,
        in_specs=(P("row", "col"), P(), P(), P(), P(), P("row", "col")),
        out_specs=(P("row", "col"), P("row", "col"), P(), P(), P(), P()),
        check_vma=False,
    )
```

```python
import jax
import jax.numpy as jnp
from jax import lax
from jax.experimental import pallas as pl
from jax.experimental.pallas import tpu as pltpu
from jax.sharding import PartitionSpec as P

MESH = pl.DeviceIdType.MESH
F32 = jnp.float32
BF16 = jnp.bfloat16
CH = 64
ROWS = 32
WIDTH = 1024
QUAD = 256
INV_BINS = 1.0 / 512
PLANE = 32
DEPTH = 8
LINES = 10
SLOPE = 0.7978845608
CUBIC = 0.044715
AROUND = tuple((a, b) for a in (-1, 0, 1) for b in (-1, 0, 1) if a or b)
ENDS = {-1: (pl.ds(1, 1), pl.ds(5, 1)), 0: (pl.ds(1, 4), pl.ds(1, 4)), 1: (pl.ds(4, 1), pl.ds(0, 1))}
SIDES = {-1: (pl.ds(1, 1), pl.ds(3, 1)), 0: (pl.ds(1, 2), pl.ds(1, 2)), 1: (pl.ds(2, 1), pl.ds(0, 1))}


def plane_id(row, col, peer):
    return (lax.rem(peer, 2) * 8 + lax.rem(row, 8), (peer // 2) * 2 + lax.rem(col, 2))


def depth_id(row, col, peer):
    return ((row // 8) * 8 + peer, col)


def block_of(taps, transpose):
    zero = jnp.zeros((CH, CH), F32)
    value = taps.astype(F32)
    if transpose:
        value = value.T
    left = jnp.concatenate([value, zero], axis=1).astype(BF16)
    right = jnp.concatenate([zero, value], axis=1).astype(BF16)
    return left, right


def fill(matrix, taps_ref, flip):
    matrix[...] = jnp.zeros(matrix.shape, BF16)
    for a in range(3):
        for b in range(3):
            if flip:
                left, right = block_of(taps_ref[2 - a, 2 - b], True)
            else:
                left, right = block_of(taps_ref[a, b], False)
            for k in range(4):
                rows = pl.ds(b * QUAD + k * CH, CH)
                cols = pl.ds(a * QUAD + (k // 2) * 128, 128)
                matrix[rows, cols] = right if k % 2 else left


def pack(own, padded):
    for q in range(4):
        for g in range(2):
            rows = own[8 * q : 8 * q + 8]
            pair = [rows[:, QUAD * (2 * g + s) : QUAD * (2 * g + s + 1)] for s in range(2)]
            padded[q + 1, g + 1] = jnp.concatenate(pair, axis=0).astype(BF16)


def unpack(padded):
    values = padded[...].astype(F32)
    return [
        jnp.concatenate([values[q, g // 2, 8 * (g % 2) : 8 * (g % 2) + 8] for q in range(6)], axis=0)
        for g in range(8)
    ]


def clear_edges(padded, row, col):
    @pl.when(row == 0)
    def _():
        padded[0] = jnp.zeros((4, 16, QUAD), BF16)

    @pl.when(row == 15)
    def _():
        padded[5] = jnp.zeros((4, 16, QUAD), BF16)

    @pl.when(col == 0)
    def _():
        padded[:, 0] = jnp.zeros((6, 16, QUAD), BF16)

    @pl.when(col == 31)
    def _():
        padded[:, 3] = jnp.zeros((6, 16, QUAD), BF16)


def conv(groups, matrix, rows):
    count = len(groups) - 2
    groups = [group.astype(BF16) for group in groups]
    left = jnp.concatenate([jnp.stack(groups[b : b + count]) for b in range(3)], axis=-1)
    full = jnp.dot(left.reshape(count * 48, 3 * QUAD), matrix[...], preferred_element_type=F32)
    full = full.reshape(count, 48, 3 * QUAD)
    return (
        full[:, 0:rows, 0:QUAD]
        + full[:, 4 : 4 + rows, QUAD : 2 * QUAD]
        + full[:, 8 : 8 + rows, 2 * QUAD :]
    )


def spread(own, matrix):
    left = own.reshape(128, QUAD).astype(BF16)
    columns = []
    for b in range(3):
        full = jnp.dot(left, matrix[b * QUAD : (b + 1) * QUAD], preferred_element_type=F32).reshape(4, 32, 3 * QUAD)
        lower, upper = jnp.zeros((4, 4, QUAD), F32), jnp.zeros((4, 8, QUAD), F32)
        columns.append(
            jnp.concatenate([upper, full[:, :, :QUAD]], axis=1)
            + jnp.concatenate([lower, full[:, :, QUAD : 2 * QUAD], lower], axis=1)
            + jnp.concatenate([full[:, :, 2 * QUAD :], upper], axis=1)
        )
    out = []
    for g in range(6):
        terms = [columns[b][g - 2 + b] for b in range(3) if 0 <= g - 2 + b < 4]
        out.append(sum(terms[1:], terms[0]))
    return jnp.stack(out)


def windows(groups, count, rows, turned_rows):
    for a in range(3):
        for b in range(3):
            window = jnp.concatenate([groups[g][4 * a : 4 * a + rows] for g in range(b, b + count)], axis=0)
            turned_rows[pl.ds(QUAD * (3 * a + b), QUAD), 0 : count * rows] = window.astype(BF16).T


def halves(full, tap):
    one = full[tap * QUAD : (tap + 1) * QUAD, :128]
    two = full[tap * QUAD : (tap + 1) * QUAD, 128:]
    return one[0:64] + two[128:192], one[64:128] + two[192:256]


def turned(block, spare, base):
    lane = lax.broadcasted_iota(jnp.int32, (8, 128), 1)
    for p in range(8):
        spare[pl.ds(base + 16 * p, 16), :] = block[:, 128 * p : 128 * p + 128]
    for p in range(8):
        even = spare[pl.ds(base + 16 * p, 8, stride=2), :]
        odd = spare[pl.ds(base + 16 * p + 1, 8, stride=2), :]
        spare[pl.ds(base + 128 + 16 * p, 8), :] = jnp.where(lane < 64, even, pltpu.roll(odd, 64, 1))
        spare[pl.ds(base + 128 + 16 * p + 8, 8), :] = jnp.where(lane < 64, pltpu.roll(even, 64, 1), odd)
    return jnp.concatenate([spare[pl.ds(base + 128 + q, 16, stride=8), :] for q in range(8)], axis=1)


def grouped(tile):
    return jnp.stack([tile[:, QUAD * g : QUAD * (g + 1)] for g in range(4)])


def kernel(
    act_hbm, cot_hbm, one_hbm, two_hbm, bias_one_hbm, bias_two_hbm,
    sym_out, grad_out, full,
    act, cot, one, two, bias_one, bias_two, mat_one, mat_two, back_one, back_two,
    source_pad, sym_pad, mirror, summed, relay, mirror_sum, spare,
    hidden_turned, source_turned, parts, core_in, plane_in, depth_in,
    load_sem, m_send, m_recv, s_send, s_recv, r_send, r_recv, x_send, x_recv, g_send, g_recv, ar_send, ar_recv,
):
    row, col = lax.axis_index("row"), lax.axis_index("col")
    core = lax.rem(col, 2)
    plane = (col // 2) * 2 + row // 8
    depth = lax.rem(row, 8)
    sibling = (row, col + 1 - 2 * core)
    around = [(lax.rem(row + a + 16, 16), lax.rem(col + b + 32, 32)) for a, b in AROUND]
    opposite = [(col // 2, 2 * row + h) for h in range(2)]
    diagonal = col // 2 == row
    is_self = [diagonal & (core == h) for h in range(2)]

    loads = [
        pltpu.make_async_copy(src, dst, load_sem.at[k])
        for k, (src, dst) in enumerate((
            (act_hbm, act), (one_hbm, one), (two_hbm, two), (cot_hbm, cot), (bias_one_hbm, bias_one), (bias_two_hbm, bias_two)
        ))
    ]
    for copy in loads:
        copy.start()
    barrier = pltpu.get_barrier_semaphore()
    for h in range(2):
        @pl.when(jnp.logical_not(is_self[h]))
        def _():
            pl.semaphore_signal(barrier, inc=1, device_id=opposite[h], device_id_type=MESH)
    for device in around + [sibling]:
        pl.semaphore_signal(barrier, inc=1, device_id=device, device_id_type=MESH)

    @pl.loop(1, PLANE)
    def _(step):
        pl.semaphore_signal(barrier, inc=1, device_id=plane_id(row, col, lax.rem(plane + step, PLANE)), device_id_type=MESH)

    @pl.loop(1, DEPTH)
    def _(step):
        pl.semaphore_signal(barrier, inc=1, device_id=depth_id(row, col, lax.rem(depth + step, DEPTH)), device_id_type=MESH)

    loads[0].wait()
    source = act[...].astype(F32)
    pack(source, source_pad)

    def swap_start(src, dst, send, recv):
        for h in range(2):
            @pl.when(jnp.logical_not(is_self[h]))
            def _():
                for k in range(2):
                    lanes = pl.ds(512 * k, 512)
                    pltpu.make_async_remote_copy(
                        src_ref=src.at[pl.ds(16 * h, 16), lanes], dst_ref=dst.at[core, :, lanes], send_sem=send.at[h], recv_sem=recv.at[core],
                        device_id=opposite[h], device_id_type=MESH,
                    ).start()

            @pl.when(is_self[h])
            def _():
                pltpu.make_async_copy(src.at[pl.ds(16 * h, 16)], dst.at[core], recv.at[core]).start()

    def swap_sent(src, dst, send):
        for h in range(2):
            @pl.when(jnp.logical_not(is_self[h]))
            def _():
                pltpu.make_async_copy(src.at[pl.ds(16 * h, 16)], dst.at[h], send.at[h]).wait()

    def halo_start(padded, send, recv):
        copies = []
        for k, (a, b) in enumerate(AROUND):
            copies.append(
                pltpu.make_async_remote_copy(
                    src_ref=padded.at[ENDS[a][0], SIDES[b][0]], dst_ref=padded.at[ENDS[a][1], SIDES[b][1]],
                    send_sem=send.at[k], recv_sem=recv.at[k], device_id=around[k], device_id_type=MESH,
                )
            )
            copies[-1].start()
        return copies

    loads[3].wait()
    pl.semaphore_wait(barrier, 2 + 8 + 1 + PLANE - 1 + DEPTH - 1 - diagonal.astype(jnp.int32))
    swap_start(cot, mirror, m_send, m_recv)
    source_halo = halo_start(source_pad, s_send, s_recv)

    for k in (1, 2, 4, 5):
        loads[k].wait()
    fill(mat_one, one, False)
    fill(mat_two, two, False)
    fill(back_two, two, True)
    fill(back_one, one, True)
    parts[8:CH, 9, :] = jnp.zeros((CH - 8, 128), F32)

    line = lax.broadcasted_iota(jnp.int32, (40, QUAD), 0)
    inside = ((line >= 4) | (row > 0)) & ((line < 36) | (row < 15))
    first = inside & (col > 0)
    last = inside & (col < 31)

    def masked(values):
        return jnp.stack([jnp.where((first, inside, inside, inside, inside, last)[g], values[g], 0.0) for g in range(6)])

    for copy in source_halo:
        copy.wait_recv()
    clear_edges(source_pad, row, col)
    source_groups = unpack(source_pad)
    wide_one = jnp.concatenate([bias_one[...]] * 4, axis=1)
    wide_two = jnp.concatenate([bias_two[...]] * 4, axis=1)
    preact = conv(source_groups, mat_one, 40) + wide_one
    bent = jnp.tanh(SLOPE * (preact + CUBIC * preact * preact * preact))
    hidden = masked(0.5 * preact * (1.0 + bent))
    slope = masked(
        0.5 * (1.0 + bent)
        + 0.5 * preact * (1.0 - bent * bent) * (SLOPE * (1.0 + 3.0 * CUBIC * preact * preact))
    )
    blank = jnp.zeros((6, 8, QUAD), F32)
    hidden = jnp.concatenate([hidden, blank], axis=1)
    hidden_groups = [hidden[g] for g in range(6)]
    branch = conv(hidden_groups, mat_two, 32) + wide_two
    summed[...] = (source + jnp.concatenate([branch[g] for g in range(4)], axis=1)).astype(BF16)

    windows(hidden_groups, 4, 32, hidden_turned)
    windows(source_groups, 6, 40, source_turned)
    source_turned[:, 240:QUAD] = jnp.zeros((9 * QUAD, 16), BF16)
    for h in range(2):
        pltpu.make_async_copy(mirror.at[h], mirror.at[h], m_recv.at[h]).wait()
    for step in range(1, DEPTH):
        pltpu.make_async_remote_copy(
            src_ref=summed.at[:, pl.ds(128 * step, 128)], dst_ref=relay.at[depth], send_sem=r_send, recv_sem=r_recv,
            device_id=depth_id(row, col, lax.rem(depth + step, DEPTH)), device_id_type=MESH,
        ).start()
    relay[depth] = summed[:, 0:128]
    turned_cot = jnp.concatenate([turned(mirror[h].astype(F32), spare, 256 * h) for h in range(2)], axis=0)
    sym = ((cot[...].astype(F32) + turned_cot) * 0.5).astype(BF16).astype(F32)

    sym_own = grouped(sym)
    share = spread(sym_own, back_two) * slope
    taps_two = jnp.dot(hidden_turned[...], sym_own.reshape(128, QUAD).astype(BF16), preferred_element_type=F32)
    rows = jnp.concatenate([share.reshape(240, QUAD), jnp.zeros((16, QUAD), F32)], axis=0).astype(BF16)
    taps_one = jnp.dot(source_turned[...], rows, preferred_element_type=F32)
    left = lax.broadcasted_iota(jnp.int32, (CH, 128), 1) < CH
    for a in range(3):
        for b in range(3):
            near_one, far_one = halves(taps_one, 3 * a + b)
            near_two, far_two = halves(taps_two, 3 * a + b)
            parts[:, 3 * a + b, :] = jnp.where(
                left, near_one + pltpu.roll(far_one, CH, 1), far_two + pltpu.roll(near_two, CH, 1)
            )
    bias = []
    for grads in (share, sym_own):
        total = jnp.sum(grads.reshape(-1, 8, QUAD), axis=0)
        total = total[:, :128] + total[:, 128:]
        bias.append(total + pltpu.roll(total, CH, 1))
    parts[0:8, 9, :] = jnp.where(left[:8], bias[0], bias[1])

    own = pl.ds(PLANE * core, PLANE)
    to_core = pltpu.make_async_remote_copy(
        src_ref=parts.at[pl.ds(PLANE * (1 - core), PLANE)], dst_ref=core_in, send_sem=ar_send.at[0], recv_sem=ar_recv.at[0],
        device_id=sibling, device_id_type=MESH,
    )
    to_core.start()
    pack(sym, sym_pad)
    sym_halo = halo_start(sym_pad, g_send, g_recv)
    to_core.wait_recv()
    core_in[...] = core_in[...] + parts[own]

    @pl.loop(1, PLANE)
    def _(step):
        peer = lax.rem(plane + step, PLANE)
        pltpu.make_async_remote_copy(
            src_ref=core_in.at[peer], dst_ref=plane_in.at[step - 1], send_sem=ar_send.at[1], recv_sem=ar_recv.at[1],
            device_id=plane_id(row, col, peer), device_id_type=MESH,
        ).start()

    pltpu.make_async_copy(relay.at[pl.ds(0, DEPTH - 1)], relay.at[pl.ds(0, DEPTH - 1)], r_recv).wait()

    @pl.loop(0, DEPTH)
    def _(origin):
        lanes = pl.ds(pl.multiple_of(128 * lax.rem(depth - origin + DEPTH, DEPTH), 128), 128)
        for h in range(2):
            src, dst = relay.at[origin, pl.ds(16 * h, 16)], mirror_sum.at[core, :, lanes]
            here = is_self[h] & (origin == depth)

            @pl.when(jnp.logical_not(here))
            def _():
                pltpu.make_async_remote_copy(
                    src_ref=src, dst_ref=dst, send_sem=x_send, recv_sem=x_recv,
                    device_id=(col // 2, 2 * (row - depth + origin) + h), device_id_type=MESH,
                ).start()

            @pl.when(here)
            def _():
                pltpu.make_async_copy(src, dst, x_recv).start()

    pltpu.make_async_copy(plane_in, plane_in, ar_recv.at[1]).wait()
    depth_in[depth] = jnp.sum(plane_in[...], axis=0) + core_in[plane]

    @pl.loop(1, DEPTH)
    def _(step):
        peer = lax.rem(depth + step, DEPTH)
        pltpu.make_async_remote_copy(
            src_ref=depth_in.at[depth], dst_ref=depth_in.at[depth], send_sem=ar_send.at[2], recv_sem=ar_recv.at[2],
            device_id=depth_id(row, col, peer), device_id_type=MESH,
        ).start()

    pltpu.make_async_copy(depth_in.at[pl.ds(0, DEPTH - 1)], depth_in.at[pl.ds(0, DEPTH - 1)], ar_recv.at[2]).wait()
    here = PLANE * core + plane
    full[here] = jnp.sum(depth_in[...], axis=0) * INV_BINS

    @pl.loop(1, PLANE)
    def _(step):
        pltpu.make_async_remote_copy(
            src_ref=full.at[here], dst_ref=full.at[here], send_sem=ar_send.at[3], recv_sem=ar_recv.at[3],
            device_id=plane_id(row, col, lax.rem(plane + step, PLANE)), device_id_type=MESH,
        ).start()

    for copy in sym_halo:
        copy.wait_recv()
    clear_edges(sym_pad, row, col)
    pre_grad = conv(unpack(sym_pad), back_two, 40) * slope
    pre_grad = jnp.concatenate([pre_grad, blank], axis=1).astype(BF16)
    input_grad = conv([pre_grad[g] for g in range(6)], back_one, 32)
    grad_out[...] = (sym + jnp.concatenate([input_grad[g] for g in range(4)], axis=1)).astype(BF16)

    pltpu.make_async_copy(plane_in, plane_in, ar_recv.at[3]).wait()
    back_core = pltpu.make_async_remote_copy(
        src_ref=full.at[own], dst_ref=full.at[own], send_sem=ar_send.at[4], recv_sem=ar_recv.at[4],
        device_id=sibling, device_id_type=MESH,
    )
    back_core.start()
    pltpu.make_async_copy(mirror_sum, mirror_sum, x_recv).wait()
    turned_sum = jnp.concatenate([turned(mirror_sum[h].astype(F32), spare, 256 * h) for h in range(2)], axis=0)
    sym_out[...] = ((summed[...].astype(F32) + turned_sum) * 0.5).astype(BF16)

    swap_sent(cot, mirror, m_send)
    pltpu.make_async_copy(relay.at[pl.ds(0, DEPTH - 1)], relay.at[pl.ds(0, DEPTH - 1)], r_send).wait()

    @pl.when(jnp.logical_not(diagonal))
    def _():
        pltpu.make_async_copy(mirror_sum, mirror_sum, x_send).wait()

    @pl.when(diagonal)
    def _():
        piece = mirror_sum.at[0, :, pl.ds(0, 7 * 128)]
        pltpu.make_async_copy(mirror_sum.at[1], mirror_sum.at[1], x_send).wait()
        pltpu.make_async_copy(piece, piece, x_send).wait()

    for copy in source_halo + sym_halo + [to_core]:
        copy.wait_send()
    pltpu.make_async_copy(plane_in, plane_in, ar_send.at[1]).wait()
    pltpu.make_async_copy(depth_in.at[pl.ds(0, DEPTH - 1)], depth_in.at[pl.ds(0, DEPTH - 1)], ar_send.at[2]).wait()
    pltpu.make_async_copy(plane_in, plane_in, ar_send.at[3]).wait()
    back_core.wait()


def unfold(sym, grad, full, sym_out, grad_out, one_out, bias_one_out, two_out, bias_two_out, one, two, bias_one, bias_two, sems):
    def send(k, src, dst):
        copy = pltpu.make_async_copy(src, dst, sems.at[k])
        copy.start()
        return copy

    copies = [send(0, sym, sym_out), send(1, grad, grad_out)]
    bias = jnp.sum(full[:, 9, :], axis=0, keepdims=True)
    bias_one[...] = bias[:, :CH]
    bias_two[...] = pltpu.roll(bias, CH, 1)[:, :CH]
    copies += [send(2, bias_one, bias_one_out), send(3, bias_two, bias_two_out)]
    for a in range(3):
        for b in range(3):
            tap = full[:, 3 * a + b, :]
            one[a, b] = tap[:, :CH]
            two[a, b] = pltpu.roll(tap, CH, 1)[:, :CH]
        copies += [send(4 + a, one.at[a], one_out.at[a]), send(7 + a, two.at[a], two_out.at[a])]
    for copy in copies:
        copy.wait()


def on_device(activations, conv_one, bias_one, conv_two, bias_two, cotangent):
    vmem, anywhere = pl.BlockSpec(memory_space=pltpu.VMEM), pl.BlockSpec(memory_space=pl.ANY)
    dma = pltpu.SemaphoreType.DMA
    tile = jax.ShapeDtypeStruct((ROWS, WIDTH), BF16)
    inputs = (activations, cotangent, conv_one, conv_two, bias_one.reshape(1, CH), bias_two.reshape(1, CH))
    held = pl.pallas_call(
        kernel,
        out_shape=(
            pltpu.VMEM((ROWS, WIDTH), BF16),
            pltpu.VMEM((ROWS, WIDTH), BF16),
            pltpu.VMEM((CH, LINES, 128), F32),
        ),
        in_specs=[anywhere] * 6,
        out_specs=[vmem] * 3,
        scratch_shapes=[
            pltpu.VMEM((ROWS, WIDTH), BF16),
            pltpu.VMEM((ROWS, WIDTH), BF16),
            pltpu.VMEM((3, 3, CH, CH), BF16),
            pltpu.VMEM((3, 3, CH, CH), BF16),
            pltpu.VMEM((1, CH), F32),
            pltpu.VMEM((1, CH), F32),
        ]
        + [pltpu.VMEM((3 * QUAD, 3 * QUAD), BF16)] * 4
        + [
            pltpu.VMEM((6, 4, 16, QUAD), BF16),
            pltpu.VMEM((6, 4, 16, QUAD), BF16),
            pltpu.VMEM((2, 16, WIDTH), BF16),
            pltpu.VMEM((ROWS, WIDTH), BF16),
            pltpu.VMEM((DEPTH, ROWS, 128), BF16),
            pltpu.VMEM((2, 16, WIDTH), BF16),
            pltpu.VMEM((512, 128), F32),
            pltpu.VMEM((9 * QUAD, 128), BF16),
            pltpu.VMEM((9 * QUAD, QUAD), BF16),
            pltpu.VMEM((CH, LINES, 128), F32),
            pltpu.VMEM((PLANE, LINES, 128), F32),
            pltpu.VMEM((PLANE - 1, LINES, 128), F32),
            pltpu.VMEM((DEPTH, LINES, 128), F32),
            dma((6,)), dma((2,)), dma((2,)), dma((8,)), dma((8,)), dma, dma, dma, dma, dma((8,)), dma((8,)), dma((5,)), dma((5,)),
        ],
        compiler_params=pltpu.CompilerParams(collective_id=0, has_side_effects=True, vmem_limit_bytes=48 * 1024 * 1024),
    )(*(pltpu.with_memory_space_constraint(x, pltpu.HBM) for x in inputs))
    taps = jax.ShapeDtypeStruct((3, 3, CH, CH), F32)
    bias = jax.ShapeDtypeStruct((1, CH), F32)
    symmetric_out, input_grad, grad_w1, grad_b1, grad_w2, grad_b2 = pl.pallas_call(
        unfold,
        out_shape=(tile, tile, taps, bias, taps, bias),
        in_specs=[vmem] * 3,
        out_specs=[anywhere] * 6,
        scratch_shapes=[pltpu.VMEM((3, 3, CH, CH), F32)] * 2 + [pltpu.VMEM((1, CH), F32)] * 2 + [dma((10,))],
        compiler_params=pltpu.CompilerParams(vmem_limit_bytes=8 * 1024 * 1024),
    )(*(pltpu.with_memory_space_constraint(x, pltpu.VMEM) for x in held))
    return symmetric_out, input_grad, grad_w1, grad_b1.reshape(CH), grad_w2, grad_b2.reshape(CH)


def solution(mesh):
    return jax.shard_map(
        on_device,
        mesh=mesh,
        in_specs=(P("row", "col"), P(), P(), P(), P(), P("row", "col")),
        out_specs=(P("row", "col"), P("row", "col"), P(), P(), P(), P()),
        check_vma=False,
    )
```
